256 devices in a mesh: wide: 64 (over x, z, core), narrow: 4 (over y).
Axes of the slice: x: 4, y: 4, z: 8, core: 2. Of those that a mesh axis runs over, the one named last changes fastest.
Arguments:
- node_features: bfloat16 [524288, 256], P(('wide', 'narrow'))
- query_weight: bfloat16 [256, 256], replicated, may hold values from -0.375 to 0.375
- key_weight: bfloat16 [256, 256], replicated, may hold values from -0.375 to 0.375
- value_weight: bfloat16 [256, 256], replicated, may hold values from -0.375 to 0.375
- graph_weight: bfloat16 [256, 256], replicated, may hold values from -0.375 to 0.375
- norm_gain: float32 [256], replicated, may hold values from 0.5 to 1.5
- tile_values: bfloat16 [24576, 128, 128], P(('wide', 'narrow')), may hold values from -0.21875 to 0.21875
- tile_rows: int32 [256, 96], P(('wide', 'narrow')), may hold values from 0 to 15
- tile_cols: int32 [256, 96], P(('wide', 'narrow')), may hold values from 0 to 127
- tile_count: int32 [256], P(('wide', 'narrow')), may hold values from 24 to 96, as said below
- send_list: int32 [256, 64], P(('wide', 'narrow')), may hold values from -1 to 15
Outputs:
- layer_out: bfloat16 [524288, 256], P(('wide', 'narrow'))
The draws below stay inside these ranges and needn't reach their ends.
Inputs may be any that keep to these rules, and one draw needn't show every extreme that they name: `tile_count`: on one device some slots are live up to the full 96. `send_list`: entry [s, j] names one of device s's 16 row blocks, or -1. `tile_cols`: index into the 128 column blocks of the device's column space.
All inputs are finite; a program needn't handle non-finite values.
Results may differ from the reference program's by a relative error of at most 0.0055.
Values may be sent and summed in bfloat16 or wider, within the bound.
No kernel may reach another device: no remote copies, remote signals or barrier semaphores. Data moves between devices by JAX's collectives and lax.ppermute only.
A program may use at most 128 MiB of HBM per device.

```python
import math
import jax
import jax.numpy as jnp
from jax import lax

D = 256
BLOCK = 128
RB = 16
TPB = 6
TILES = 96
ROWS_DEV = 2048
ROWS = 524288
COLS = 128
N_WIDE = 64
N_NARROW = 4
DEVICES = 256


def draw_node_features(key, part):
    key = jax.random.fold_in(key, 11)
    key_a, key_b, key_c, key_d, key_e, key_f, key_g = jax.random.split(key, 7)
    device_pos = jnp.arange(DEVICES, dtype=jnp.float32) / max(DEVICES - 1, 1)
    rising = jnp.exp(device_pos * math.log(3.0)) * jnp.exp(jax.random.uniform(key_f, (DEVICES,), jnp.float32) * math.log(2.0))
    column_scale = jnp.exp(jax.random.uniform(key_d, (D,), jnp.float32) * math.log(10.0))
    heavy_device = jax.random.randint(key_e, (), 0, DEVICES)
    boost = jnp.where(jnp.arange(DEVICES, dtype=jnp.int32) == heavy_device, 4.0, 1.0).astype(jnp.float32)
    rough = jax.random.normal(key_a, (DEVICES, ROWS_DEV, D), jnp.float32)
    center = 0.7 * jax.random.normal(key_b, (D,), jnp.float32)
    device_center = 0.8 * jax.random.normal(key_g, (DEVICES, D), jnp.float32)
    row_scale = jnp.exp(jax.random.uniform(key_c, (DEVICES, ROWS_DEV, 1), jnp.float32) * math.log(10.0))
    mixed = center[None, None, :] + device_center[:, None, :] + rough
    values = mixed * row_scale * (rising * boost)[:, None, None] * column_scale[None, None, :] / 10.0
    return values.reshape(ROWS, D).astype(jnp.bfloat16)


def draw_tile_count(key, part):
    key = jax.random.fold_in(key, 5)
    key_a, key_b = jax.random.split(key)
    counts = jax.random.randint(key_a, (DEVICES,), TILES // 4, TILES + 1)
    fullest = jax.random.randint(key_b, (), 0, DEVICES)
    return counts.at[fullest].set(TILES).astype(jnp.int32)


def place_ends(drawn, own_key, low, largest):
    spot = [jax.random.randint(jax.random.fold_in(own_key, axis), (), 0, length) for axis, length in enumerate(drawn.shape)]
    longest = drawn.shape.index(max(drawn.shape))
    beside = spot[:longest] + [(spot[longest] + 1) % drawn.shape[longest]] + spot[longest + 1:]
    return drawn.at[tuple(spot)].set(low).at[tuple(beside)].set(largest)


def shard_levels(rng, dims, cuts, least, largest):
    loudness, own = 1.0, jax.random.fold_in(rng, 6)
    for dim, shards_of in cuts:
        heights = jnp.exp(jax.random.uniform(jax.random.fold_in(own, dim), (shards_of,), jnp.float32, least / len(cuts), largest / len(cuts)))
        loudness = loudness * jnp.repeat(heights, dims[dim] // shards_of).reshape([-1 if axis == dim else 1 for axis in range(len(dims))])
    return loudness


def gaussian(own_key, dims, scale, limit, cuts=(), kind=jnp.bfloat16):
    values = scale * jax.random.normal(own_key, dims, jnp.float32)
    if cuts:
        values = values * shard_levels(own_key, dims, cuts, -0.22, 0.18)
    return jnp.clip(values, -limit, limit).astype(kind)


def setup_inputs(seed: int = 0) -> dict:
    key_list = jax.random.split(jax.random.key(seed), 12)
    return {
        "node_features": draw_node_features(jax.random.fold_in(key_list[11], 71), 0),
        "query_weight": gaussian(key_list[1], (D, D), D ** -0.5, 0.375),
        "key_weight": gaussian(key_list[2], (D, D), D ** -0.5, 0.375),
        "value_weight": gaussian(key_list[3], (D, D), D ** -0.5, 0.375),
        "graph_weight": gaussian(key_list[4], (D, D), D ** -0.5, 0.375),
        "norm_gain": jnp.clip(1.0 + 0.1 * jax.random.normal(key_list[5], (D,), jnp.float32), 0.5, 1.5),
        "tile_values": gaussian(key_list[6], (DEVICES * TILES, BLOCK, BLOCK), (BLOCK * TPB) ** -0.5, 0.21875, ((0, 256),)),
        "tile_rows": place_ends(jax.random.randint(key_list[7], (DEVICES, TILES), 0, RB), jax.random.fold_in(key_list[7], 1), 0, RB - 1).astype(jnp.int32),
        "tile_cols": place_ends(jax.random.randint(key_list[8], (DEVICES, TILES), 0, COLS), jax.random.fold_in(key_list[8], 1), 0, COLS - 1).astype(jnp.int32),
        "tile_count": draw_tile_count(jax.random.fold_in(key_list[11], 71), 0),
        "send_list": place_ends(jax.random.randint(key_list[10], (DEVICES, N_WIDE), -1, RB), jax.random.fold_in(key_list[10], 1), -1, RB - 1).astype(jnp.int32),
    }


def reference(node_features, query_weight, key_weight, value_weight, graph_weight, norm_gain, tile_values, tile_rows, tile_cols, tile_count, send_list):
    highest = lax.Precision.HIGHEST
    total = float(ROWS)
    width = float(D)
    spans = node_features.reshape(DEVICES, ROWS_DEV, D)

    def project(span):
        query = jnp.dot(span, query_weight, preferred_element_type=jnp.float32)
        keys = jnp.dot(span, key_weight, preferred_element_type=jnp.float32)
        values = jnp.dot(span, value_weight, preferred_element_type=jnp.float32)
        return (query, keys, values)

    def squares(span):
        query, keys, values = project(span)
        return (jnp.sum(query * query), jnp.sum(keys * keys))
    query_parts, key_parts = lax.map(squares, spans)
    query_sq = jnp.sum(query_parts)
    key_sq = jnp.sum(key_parts)

    def sums(span):
        query, keys, values = project(span)
        key_feat = keys * keys * (total * width / key_sq)
        return (jnp.dot(key_feat.T, values, precision=highest), lax.optimization_barrier(jnp.sum(key_feat, 0)))
    kv_parts, ks_parts = lax.map(sums, spans)
    kv_mean = lax.optimization_barrier(jnp.sum(kv_parts, 0)) / total
    key_mean = lax.optimization_barrier(jnp.sum(ks_parts, 0)) / total

    def graph_project(span):
        return jnp.dot(span, graph_weight, preferred_element_type=jnp.float32).astype(jnp.bfloat16)
    hop_zero = lax.map(graph_project, spans).reshape(ROWS, D)
    values_t = tile_values.reshape(DEVICES, TILES, BLOCK, BLOCK)

    def propagate(field):
        blocks = jnp.concatenate([field.reshape(ROWS // BLOCK, BLOCK, D), jnp.zeros((1, BLOCK, D), jnp.bfloat16)], 0)
        zero_index = ROWS // BLOCK

        def one_device(inputs):
            dev, tiles, rows, cols, count = inputs
            wide_at = dev // N_NARROW
            narrow_at = dev % N_NARROW
            local = cols < N_NARROW * RB
            local_index = (wide_at * N_NARROW + cols // RB) * RB + cols % RB
            peer = jnp.clip(cols - N_NARROW * RB, 0, N_WIDE - 1)
            sender = peer * N_NARROW + narrow_at
            entry = send_list[sender, wide_at]
            halo_index = jnp.where(entry < 0, zero_index, sender * RB + entry)
            index = jnp.where(local, local_index, halo_index).astype(jnp.int32)
            gathered = jnp.take(blocks, index, axis=0)
            prod = jnp.einsum('tij,tjd->tid', tiles.astype(jnp.float32), gathered.astype(jnp.float32), precision=highest)
            active = jnp.arange(TILES, dtype=jnp.int32) < count
            onehot = ((rows[None, :] == jnp.arange(RB, dtype=jnp.int32)[:, None]) & active[None, :]).astype(jnp.float32)
            out = jnp.einsum('rt,tid->rid', onehot, prod, precision=highest)
            return out.reshape(ROWS_DEV, D).astype(jnp.bfloat16)
        result = lax.map(one_device, (jnp.arange(DEVICES, dtype=jnp.int32), values_t, tile_rows, tile_cols, tile_count))
        return result.reshape(ROWS, D)
    hop_one = propagate(hop_zero)
    hop_two = propagate(hop_one)
    hops = (hop_zero.reshape(DEVICES, ROWS_DEV, D), hop_one.reshape(DEVICES, ROWS_DEV, D), hop_two.reshape(DEVICES, ROWS_DEV, D))

    def finish(inputs):
        span, first, second, third = inputs
        query, keys, values = project(span)
        query_feat = query * query * (total * width / query_sq)
        numer = jnp.dot(query_feat, kv_mean, precision=highest) + width * values
        denom = lax.optimization_barrier(jnp.sum(query_feat * key_mean[None, :], 1, keepdims=True)) + width
        attention = numer / denom
        mixed = attention + (first.astype(jnp.float32) + second.astype(jnp.float32) + third.astype(jnp.float32)) / 3.0
        center = mixed - lax.optimization_barrier(jnp.mean(mixed, 1, keepdims=True))
        scale = lax.rsqrt(lax.optimization_barrier(jnp.mean(center * center, 1, keepdims=True)) + 1e-05)
        return (norm_gain[None, :] * center * scale).astype(jnp.bfloat16)
    out = lax.map(finish, (spans,) + hops)
    return out.reshape(ROWS, D)
```

```python
import functools

import jax
import jax.numpy as jnp
from jax import lax
from jax.experimental import pallas as pl
from jax.experimental.pallas import tpu as pltpu
from jax.sharding import PartitionSpec as P

D = 256
BLOCK = 128
UNROLL = 8
CHUNK = 256
F32 = jnp.float32
BF16 = jnp.bfloat16
HIGHEST = lax.Precision.HIGHEST
SMEM = pl.BlockSpec(memory_space=pltpu.SMEM)
VMEM = pl.BlockSpec(memory_space=pltpu.VMEM)
ANY = pl.BlockSpec(memory_space=pl.ANY)


def params(mib):
    return pltpu.CompilerParams(vmem_limit_bytes=mib << 20)


def cost(flops, nbytes):
    return pl.CostEstimate(flops=flops, bytes_accessed=nbytes, transcendentals=0)


def send_blocks(send, src, zeros, out, sem):
    zeros[...] = jnp.zeros_like(zeros)

    def one(w, _):
        index = send[0, w]

        @pl.when(index >= 0)
        def _():
            pltpu.make_async_copy(src.at[jnp.maximum(index, 0)], out.at[w], sem).start()

        @pl.when(index < 0)
        def _():
            pltpu.make_async_copy(zeros, out.at[w], sem).start()

        return 0

    lax.fori_loop(0, out.shape[0], one, 0)
    pltpu.make_async_copy(out, out, sem).wait()


def start_kernel(send, x, weight, h_ref, out, zeros, sem):
    def one(b, _):
        rows = pl.ds(pl.multiple_of(b * BLOCK, BLOCK), BLOCK)
        h_ref[b] = jnp.dot(x[rows, :], weight[...], preferred_element_type=F32).astype(BF16)
        return 0

    lax.fori_loop(0, h_ref.shape[0], one, 0, unroll=True)
    send_blocks(send, h_ref, zeros, out, sem)


def start(send, x, weight, peers):
    nblocks = x.shape[0] // BLOCK
    return pl.pallas_call(
        start_kernel,
        out_shape=(
            jax.ShapeDtypeStruct((nblocks, BLOCK, D), BF16),
            jax.ShapeDtypeStruct((peers, BLOCK, D), BF16),
        ),
        in_specs=[SMEM, VMEM, VMEM],
        out_specs=(VMEM, ANY),
        scratch_shapes=[pltpu.VMEM((BLOCK, D), BF16), pltpu.SemaphoreType.DMA],
        compiler_params=params(16),
        name="project_send",
    )(send, x, weight)


def stats_kernel(x, qw, kw, vw, out, keys_sq, values, sums):
    steps = x.shape[0] // CHUNK
    ksum = jnp.zeros((1, D), F32)
    qsum = jnp.zeros((1, D), F32)
    for c in range(steps):
        rows = pl.ds(c * CHUNK, CHUNK)
        part = x[rows, :]
        query = jnp.dot(part, qw[...], preferred_element_type=F32)
        keys = jnp.dot(part, kw[...], preferred_element_type=F32)
        values[rows, :] = jnp.dot(part, vw[...], preferred_element_type=F32)
        keys_sq[rows, :] = keys * keys
        ksum = ksum + jnp.sum(keys * keys, 0, keepdims=True)
        qsum = qsum + jnp.sum(query * query, 0, keepdims=True)
    ktotal = jnp.sum(ksum, 1, keepdims=True)
    qtotal = jnp.sum(qsum, 1, keepdims=True)
    divisor = jnp.where(ktotal > 0, ktotal, 1.0)
    sums[...] = jnp.zeros_like(sums)

    def one(c, _):
        rows = pl.ds(pl.multiple_of(c * CHUNK, CHUNK), CHUNK)
        feat = keys_sq[rows, :] / divisor
        sums[...] += lax.dot_general(
            feat, values[rows, :], (((0,), (0,)), ((), ())),
            precision=HIGHEST, preferred_element_type=F32,
        )
        return 0

    lax.fori_loop(0, steps, one, 0)
    peers = out.shape[0]
    each = D // peers
    out[:, 4:5, :] = jnp.broadcast_to((ksum / divisor)[None], (peers, 1, D))
    out[:, 5:6, :] = jnp.broadcast_to(ktotal[None], (peers, 1, D))
    out[:, 6:7, :] = jnp.broadcast_to(qtotal[None], (peers, 1, D))
    out[:, 7:8, :] = jnp.zeros((peers, 1, D), F32)
    for w in range(peers):
        out[w, 0:each, :] = sums[w * each:(w + 1) * each, :]


def stats(x, qw, kw, vw, peers):
    rows = x.shape[0]
    return pl.pallas_call(
        stats_kernel,
        out_shape=jax.ShapeDtypeStruct((peers, 8, D), F32),
        in_specs=[VMEM] * 4,
        out_specs=VMEM,
        scratch_shapes=[pltpu.VMEM((rows, D), F32)] * 2 + [pltpu.VMEM((D, D), F32)],
        compiler_params=params(24),
        cost_estimate=cost(rows * D * D * 18, 2 << 20),
        name="attention_sums",
    )(x, qw, kw, vw)


def merge(parts):
    total = jnp.sum(parts[:, 5:6, :], 0, keepdims=True)
    weight = parts[:, 5:6, :] / jnp.where(total > 0, total, 1.0)
    means = jnp.sum(parts[:, :5, :] * weight, 0)
    return jnp.concatenate([means, total[0], jnp.sum(parts[:, 6:7, :], 0), jnp.zeros((1, D), F32)], 0)


def all_sums(parts):
    received = lax.all_to_all(parts, "wide", 0, 0, tiled=True)
    mine = merge(received)
    for step in (1, 2):
        other = lax.ppermute(mine, "narrow", [(i, i ^ step) for i in range(lax.axis_size("narrow"))])
        mine = merge(jnp.stack([mine, other]))
    return lax.all_to_all(jnp.broadcast_to(mine[None], parts.shape), "wide", 0, 0, tiled=True)


def collect(rows, cols, count, first, last, spare, lists):
    slots, places, targets = lists

    def one(t, n):
        c = cols[0, t]
        slots[n] = t
        places[n] = c - first
        targets[n] = rows[0, t]
        return n + ((c >= first) & (c < last)).astype(jnp.int32)

    n = lax.fori_loop(0, count[0], one, jnp.int32(0))
    for u in range(UNROLL):
        slots[n + u] = 0
        places[n + u] = 0
        targets[n + u] = spare
    return n


def add_tiles(n, lists, tiles, blocks, acc):
    slots, places, targets = lists

    def step(i, _):
        prods = [
            jnp.dot(tiles[slots[i * UNROLL + u]], blocks[places[i * UNROLL + u]], preferred_element_type=F32)
            for u in range(UNROLL)
        ]
        for u in range(UNROLL):
            r = targets[i * UNROLL + u]
            acc[r] = acc[r] + prods[u]
        return 0

    lax.fori_loop(0, (n + UNROLL - 1) // UNROLL, step, 0)


def local_kernel(rows, cols, count, tiles, blocks, acc, *lists):
    n = collect(rows, cols, count, 0, blocks.shape[0], acc.shape[0] - 1, lists)
    acc[...] = jnp.zeros_like(acc)
    add_tiles(n, lists, tiles, blocks, acc)


def lists_of(rows):
    return [pltpu.SMEM((rows.shape[1] + UNROLL,), jnp.int32)] * 3


def local_tiles(rows, cols, count, tiles, blocks, nblocks):
    return pl.pallas_call(
        local_kernel,
        out_shape=jax.ShapeDtypeStruct((nblocks + 1, BLOCK, D), F32),
        in_specs=[SMEM, SMEM, SMEM, VMEM, VMEM],
        out_specs=VMEM,
        scratch_shapes=lists_of(rows),
        compiler_params=params(24),
        cost_estimate=cost(48 * BLOCK * BLOCK * D * 2, 9 << 20),
        name="local_tiles",
    )(rows, cols, count, tiles, blocks)


def hop_kernel(first, send, rows, cols, count, tiles, blocks, part, h_ref, out, acc, zeros, sem, *lists):
    nblocks = h_ref.shape[0]
    n = collect(rows, cols, count, first, first + blocks.shape[0], nblocks, lists)
    acc[...] = part[...]
    add_tiles(n, lists, tiles, blocks, acc)
    h_ref[...] = acc[:nblocks].astype(BF16)
    send_blocks(send, h_ref, zeros, out, sem)


def hop(send, rows, cols, count, tiles, blocks, part, first):
    nblocks = part.shape[0] - 1
    return pl.pallas_call(
        functools.partial(hop_kernel, first),
        out_shape=(
            jax.ShapeDtypeStruct((nblocks, BLOCK, D), BF16),
            jax.ShapeDtypeStruct(blocks.shape, BF16),
        ),
        in_specs=[SMEM] * 4 + [VMEM] * 3,
        out_specs=(VMEM, ANY),
        scratch_shapes=[
            pltpu.VMEM(part.shape, F32),
            pltpu.VMEM((BLOCK, D), BF16),
            pltpu.SemaphoreType.DMA,
        ] + lists_of(rows),
        compiler_params=params(32),
        name="halo_tiles_send",
    )(send, rows, cols, count, tiles, blocks, part)


def attention_kernel(total, x, qw, vw, kv, key_mean, query_sq, hop_zero, hop_one, out):
    width = float(D)
    scale = total * width / query_sq[...]
    for c in range(x.shape[0] // CHUNK):
        rows = pl.ds(c * CHUNK, CHUNK)
        part = x[rows, :]
        query = jnp.dot(part, qw[...], preferred_element_type=F32)
        values = jnp.dot(part, vw[...], preferred_element_type=F32)
        feat = query * query * scale
        numer = jnp.dot(feat, kv[...], precision=HIGHEST, preferred_element_type=F32) + width * values
        denom = jnp.sum(feat * key_mean[...], 1, keepdims=True) + width
        graph = hop_zero[rows, :].astype(F32) + hop_one[rows, :].astype(F32)
        out[rows, :] = numer / denom + graph / 3.0


def attention(total, x, qw, vw, kv, key_mean, query_sq, hop_zero, hop_one):
    rows = x.shape[0]
    return pl.pallas_call(
        functools.partial(attention_kernel, total),
        out_shape=jax.ShapeDtypeStruct((rows, D), F32),
        in_specs=[VMEM] * 8,
        out_specs=VMEM,
        compiler_params=params(24),
        cost_estimate=cost(rows * D * D * 18, 6 << 20),
        name="attention",
    )(x, qw, vw, kv, key_mean, query_sq, hop_zero, hop_one)


def finish_kernel(first, rows, cols, count, tiles, blocks, part, base, gain, out, acc, *lists):
    nblocks = part.shape[0] - 1
    n = collect(rows, cols, count, first, first + blocks.shape[0], nblocks, lists)
    acc[...] = part[...]
    add_tiles(n, lists, tiles, blocks, acc)
    for b in range(nblocks):
        mixed = base[b] + acc[b].astype(BF16).astype(F32) / 3.0
        center = mixed - jnp.mean(mixed, 1, keepdims=True)
        scale = lax.rsqrt(jnp.mean(center * center, 1, keepdims=True) + 1e-05)
        out[b] = (gain[...] * center * scale).astype(BF16)


def finish(rows, cols, count, tiles, blocks, part, base, gain, first):
    nblocks = part.shape[0] - 1
    return pl.pallas_call(
        functools.partial(finish_kernel, first),
        out_shape=jax.ShapeDtypeStruct((nblocks, BLOCK, D), BF16),
        in_specs=[SMEM] * 3 + [VMEM] * 5,
        out_specs=VMEM,
        scratch_shapes=[pltpu.VMEM(part.shape, F32)] + lists_of(rows),
        compiler_params=params(32),
        name="halo_tiles_norm",
    )(rows, cols, count, tiles, blocks, part, base, gain)


def shards(x, qw, kw, vw, gw, gain, tiles, tile_rows, tile_cols, tile_count, send_list):
    rows_dev = x.shape[0]
    nblocks = rows_dev // BLOCK
    peers, groups = lax.axis_size("wide"), lax.axis_size("narrow")
    total = float(rows_dev * peers * groups)
    first = groups * nblocks

    hop_zero, outgoing = start(send_list, x, gw, peers)
    received = lax.all_to_all(outgoing, "wide", 0, 0, tiled=True)
    group = lax.all_gather(hop_zero, "narrow", axis=0, tiled=True)
    parts = stats(x, qw, kw, vw, peers)
    part = local_tiles(tile_rows, tile_cols, tile_count, tiles, group, nblocks)
    hop_one, outgoing = hop(
        send_list, tile_rows, tile_cols, tile_count, tiles, received, part, first
    )
    received = lax.all_to_all(outgoing, "wide", 0, 0, tiled=True)
    group = lax.all_gather(hop_one, "narrow", axis=0, tiled=True)
    part = local_tiles(tile_rows, tile_cols, tile_count, tiles, group, nblocks)
    sums = all_sums(parts)
    width = float(D)
    kv_mean = sums[:, :D // peers, :].reshape(D, D) * width
    key_mean = sums[0, 4:5, :] * width
    query_sq = sums[0, 6:7, :]
    base = attention(
        total, x, qw, vw, kv_mean, key_mean, query_sq,
        hop_zero.reshape(rows_dev, D), hop_one.reshape(rows_dev, D),
    )
    out = finish(
        tile_rows, tile_cols, tile_count, tiles, received, part,
        base.reshape(nblocks, BLOCK, D), gain[None, :], first,
    )
    return out.reshape(rows_dev, D)


def solution(mesh):
    return jax.shard_map(
        shards,
        mesh=mesh,
        in_specs=(
            P(("wide", "narrow"), None),
            P(),
            P(),
            P(),
            P(),
            P(),
            P(("wide", "narrow"), None, None),
            P(("wide", "narrow"), None),
            P(("wide", "narrow"), None),
            P(("wide", "narrow")),
            P(("wide", "narrow"), None),
        ),
        out_specs=P(("wide", "narrow"), None),
        check_vma=False,
    )
```

```python
import functools

import jax
import jax.numpy as jnp
from jax import lax
from jax.experimental import pallas as pl
from jax.experimental.pallas import tpu as pltpu
from jax.sharding import PartitionSpec as P

D = 256
BLOCK = 128
UNROLL = 8
CHUNK = 256
EXTRA = 8
CORE = ("wide", 0)
HALVE = (("wide", 4), ("wide", 5), ("narrow", 0), ("narrow", 1))
DEPTH = 8
F32 = jnp.float32
BF16 = jnp.bfloat16
HIGHEST = lax.Precision.HIGHEST
SMEM = pl.BlockSpec(memory_space=pltpu.SMEM)
VMEM = pl.BlockSpec(memory_space=pltpu.VMEM)
HBM = pl.BlockSpec(memory_space=pltpu.HBM)


def in_hbm(x):
    return pltpu.with_memory_space_constraint(x, pltpu.HBM)


def params(mib):
    return pltpu.CompilerParams(vmem_limit_bytes=mib << 20)


def cost(flops, nbytes):
    return pl.CostEstimate(flops=flops, bytes_accessed=nbytes, transcendentals=0)


def send_blocks(send, src, zeros, h_out, out, sems):
    own = pltpu.make_async_copy(src, h_out, sems.at[0])
    own.start()
    zeros[...] = jnp.zeros_like(zeros)

    def one(w, _):
        index = send[0, w]

        @pl.when(index >= 0)
        def _():
            pltpu.make_async_copy(src.at[jnp.maximum(index, 0)], out.at[w], sems.at[1]).start()

        @pl.when(index < 0)
        def _():
            pltpu.make_async_copy(zeros, out.at[w], sems.at[1]).start()

        return 0

    lax.fori_loop(0, out.shape[0], one, 0, unroll=8)
    own.wait()
    pltpu.make_async_copy(out, out, sems.at[1]).wait()


def start_kernel(send, x, weight, h_out, out, h_own, zeros, sems):
    def one(b, _):
        rows = pl.ds(pl.multiple_of(b * BLOCK, BLOCK), BLOCK)
        h_own[b] = jnp.dot(x[rows, :], weight[...], preferred_element_type=F32).astype(BF16)
        return 0

    lax.fori_loop(0, h_own.shape[0], one, 0, unroll=4)
    send_blocks(send, h_own, zeros, h_out, out, sems)


def start(send, x, weight, peers):
    nblocks = x.shape[0] // BLOCK
    return pl.pallas_call(
        start_kernel,
        out_shape=(pltpu.HBM((nblocks, BLOCK, D), BF16), pltpu.HBM((peers, BLOCK, D), BF16)),
        in_specs=[SMEM, VMEM, VMEM],
        out_specs=(HBM, HBM),
        scratch_shapes=[
            pltpu.VMEM((nblocks, BLOCK, D), BF16),
            pltpu.VMEM((BLOCK, D), BF16),
            pltpu.SemaphoreType.DMA((2,)),
        ],
        compiler_params=params(16),
        name="project_send",
    )(send, x, weight)


def stats_kernel(x, qw, kw, vw, after, out, keys_sq, values, sums):
    steps = x.shape[0] // CHUNK

    def project(c, carry):
        ksum, qsum = carry
        rows = pl.ds(pl.multiple_of(c * CHUNK, CHUNK), CHUNK)
        part = x[rows, :]
        query = jnp.dot(part, qw[...], preferred_element_type=F32)
        keys = jnp.dot(part, kw[...], preferred_element_type=F32)
        values[rows, :] = jnp.dot(part, vw[...], preferred_element_type=F32)
        keys_sq[rows, :] = keys * keys
        ksum = ksum + jnp.sum(keys * keys, 0, keepdims=True)
        return ksum, qsum + jnp.sum(query * query, 0, keepdims=True)

    zero = jnp.zeros((1, D), F32)
    ksum, qsum = lax.fori_loop(0, steps, project, (zero, zero))
    ktotal = jnp.sum(ksum, 1, keepdims=True)
    qtotal = jnp.sum(qsum, 1, keepdims=True)
    divisor = jnp.where(ktotal > 0, ktotal, 1.0)
    sums[...] = jnp.zeros_like(sums)

    def one(c, _):
        rows = pl.ds(pl.multiple_of(c * CHUNK, CHUNK), CHUNK)
        feat = keys_sq[rows, :] / divisor
        sums[...] += lax.dot_general(
            feat, values[rows, :], (((0,), (0,)), ((), ())),
            precision=HIGHEST, preferred_element_type=F32,
        )
        return 0

    lax.fori_loop(0, steps, one, 0)
    row = lax.broadcasted_iota(jnp.int32, (EXTRA, D), 0)
    extra = jnp.where(row == 0, ksum / divisor, jnp.where(row == 1, ktotal, qtotal))
    out[0:D, :] = sums[...]
    out[D:, :] = extra


def bit_of(step):
    axis, bit = step
    return lax.axis_index(axis) >> bit & 1


def split(rows, extra, bit, keep, away):
    half = rows.shape[0] // 2
    keep[0:half, :] = rows[pl.ds(pl.multiple_of(bit * half, 8), half), :]
    away[0:half, :] = rows[pl.ds(pl.multiple_of((1 - bit) * half, 8), half), :]
    keep[half:half + EXTRA, :] = extra
    away[half:half + EXTRA, :] = extra


def stats(x, qw, kw, vw, after):
    rows = x.shape[0]
    return pl.pallas_call(
        stats_kernel,
        out_shape=jax.ShapeDtypeStruct((D + EXTRA, D), F32),
        in_specs=[VMEM] * 4 + [HBM],
        out_specs=VMEM,
        scratch_shapes=[pltpu.VMEM((rows, D), F32)] * 2 + [pltpu.VMEM((D, D), F32)],
        compiler_params=params(16),
        cost_estimate=cost(rows * D * D * 18, 2 << 20),
        name="attention_sums",
    )(x, qw, kw, vw, after)


def merged(parts):
    rows = parts[0].shape[0] - EXTRA
    extras = [p[rows:, :] for p in parts]
    added = functools.reduce(jnp.add, extras)
    total = added[1:2, :]
    weights = [e[1:2, :] / jnp.where(total > 0, total, 1.0) for e in extras]
    row = lax.broadcasted_iota(jnp.int32, (EXTRA, D), 0)
    extra = jnp.where(row == 0, functools.reduce(jnp.add, [e * w for e, w in zip(extras, weights)]), added)
    return functools.reduce(jnp.add, [p[0:rows, :] * w for p, w in zip(parts, weights)]), extra


def halve_kernel(step, mine, other, keep, away, scratch):
    sums, extra = merged((mine, other))
    scratch[...] = sums
    split(scratch, extra, bit_of(step), keep, away)


def halve(mine, other, step):
    rows = mine.shape[0] - EXTRA
    return pl.pallas_call(
        functools.partial(halve_kernel, step),
        out_shape=(jax.ShapeDtypeStruct((rows // 2 + EXTRA, D), F32),) * 2,
        in_specs=[VMEM, VMEM],
        out_specs=(VMEM, VMEM),
        scratch_shapes=[pltpu.VMEM((rows, D), F32)],
        name="halve_sums",
    )(mine, other)


def merge_kernel(core, *refs):
    out = refs[-1]
    parts = [ref[...] for ref in refs[:-1]]
    if core:
        parts[0] = jnp.where(bit_of(CORE) == 0, parts[0], 0.0)
    sums, extra = merged(parts)
    rows = sums.shape[0]
    out[0:rows, :] = sums
    out[rows:, :] = extra


def merge(*parts, core=False):
    return pl.pallas_call(
        functools.partial(merge_kernel, core),
        out_shape=jax.ShapeDtypeStruct(parts[0].shape, F32),
        in_specs=[VMEM] * len(parts),
        out_specs=VMEM,
        name="merge_sums",
    )(*parts)


def join_kernel(step, mine, other, out):
    rows = mine.shape[0]
    at = bit_of(step)
    out[pl.ds(pl.multiple_of(at * rows, 8), rows), :] = mine[...]
    out[pl.ds(pl.multiple_of((1 - at) * rows, 8), rows), :] = other[...]


def join(mine, other, step):
    return pl.pallas_call(
        functools.partial(join_kernel, step),
        out_shape=jax.ShapeDtypeStruct((2 * mine.shape[0], D), F32),
        in_specs=[VMEM, VMEM],
        out_specs=VMEM,
        name="join_sums",
    )(mine, other)


def swap(x, step):
    axis, bit = step
    return lax.ppermute(x, axis, [(i, i ^ 1 << bit) for i in range(lax.axis_size(axis))])


def partial_sums(mine):
    keep, away = halve(mine, swap(mine, CORE), HALVE[0])
    for done, step in zip(HALVE, HALVE[1:]):
        keep, away = halve(keep, swap(away, done), step)
    return merge(keep, swap(away, HALVE[-1]))


def along_depth(mine):
    span, reach = 2 * DEPTH, DEPTH // 2

    def shift(by):
        return [
            (i, i // span * span + (i + 2 * (by + reach * (i % 2))) % span)
            for i in range(lax.axis_size("wide"))
            if by + reach * (i % 2) < DEPTH
        ]

    return [lax.ppermute(mine, "wide", shift(by)) for by in range(1, reach + 1)]


def whole_sums(mine, others):
    mine = merge(mine, *others, core=True)
    mine = merge(mine, swap(mine, CORE))
    rows, extra = mine[:-EXTRA], mine[-EXTRA:]
    for step in HALVE[::-1]:
        rows = join(rows, swap(rows, step), step)
    return rows, extra


def collect(rows, cols, count, first, last, spare, lists):
    slots, places, targets = lists

    def one(t, n):
        c = cols[0, t]
        slots[n] = t
        places[n] = c - first
        targets[n] = rows[0, t]
        return n + ((c >= first) & (c < last)).astype(jnp.int32)

    n = lax.fori_loop(0, count[0], one, jnp.int32(0))
    for u in range(UNROLL):
        slots[n + u] = 0
        places[n + u] = 0
        targets[n + u] = spare
    return n


def add_tiles(n, lists, tiles, blocks, acc):
    slots, places, targets = lists

    def step(i, _):
        prods = [
            jnp.dot(tiles[slots[i * UNROLL + u]], blocks[places[i * UNROLL + u]], preferred_element_type=F32)
            for u in range(UNROLL)
        ]
        for u in range(UNROLL):
            r = targets[i * UNROLL + u]
            acc[r] = acc[r] + prods[u]
        return 0

    lax.fori_loop(0, (n + UNROLL - 1) // UNROLL, step, 0)


def local_kernel(rows, cols, count, tiles, blocks, after, acc, *lists):
    n = collect(rows, cols, count, 0, blocks.shape[0], acc.shape[0] - 1, lists)
    acc[...] = jnp.zeros_like(acc)
    add_tiles(n, lists, tiles, blocks, acc)


def lists_of(rows):
    return [pltpu.SMEM((rows.shape[1] + UNROLL,), jnp.int32)] * 3


def local_tiles(rows, cols, count, tiles, blocks, after, nblocks):
    return pl.pallas_call(
        local_kernel,
        out_shape=pltpu.HBM((nblocks + 1, BLOCK, D), F32),
        in_specs=[SMEM, SMEM, SMEM, VMEM, VMEM, HBM],
        out_specs=VMEM,
        scratch_shapes=lists_of(rows),
        compiler_params=params(16),
        cost_estimate=cost(48 * BLOCK * BLOCK * D * 2, 9 << 20),
        name="local_tiles",
    )(rows, cols, count, tiles, blocks, after)


def hop_kernel(first, send, rows, cols, count, tiles, blocks, part, *refs):
    h_out, out, got, acc, h_own, zeros, sems, *lists = refs[DEPTH // 2:]
    loads = [pltpu.make_async_copy(blocks, got, sems.at[2]), pltpu.make_async_copy(part, acc, sems.at[3])]
    for load in loads:
        load.start()
    n = collect(rows, cols, count, first, first + blocks.shape[0], h_own.shape[0], lists)
    for load in loads:
        load.wait()
    add_tiles(n, lists, tiles, got, acc)
    h_own[...] = acc[:h_own.shape[0]].astype(BF16)
    send_blocks(send, h_own, zeros, h_out, out, sems)


def hop(send, rows, cols, count, tiles, blocks, part, after, first):
    nblocks = part.shape[0] - 1
    return pl.pallas_call(
        functools.partial(hop_kernel, first),
        out_shape=(pltpu.HBM((nblocks, BLOCK, D), BF16), pltpu.HBM(blocks.shape, BF16)),
        in_specs=[SMEM] * 4 + [VMEM, HBM, HBM] + [HBM] * len(after),
        out_specs=(HBM, HBM),
        scratch_shapes=[
            pltpu.VMEM(blocks.shape, BF16),
            pltpu.VMEM(part.shape, F32),
            pltpu.VMEM((nblocks, BLOCK, D), BF16),
            pltpu.VMEM((BLOCK, D), BF16),
            pltpu.SemaphoreType.DMA((4,)),
        ] + lists_of(rows),
        compiler_params=params(24),
        name="halo_tiles_send",
    )(send, rows, cols, count, tiles, in_hbm(blocks), in_hbm(part), *after)


def attention_kernel(total, x, qw, vw, kv_sums, extra, hop_zero, hop_one, out, kv):
    width = float(D)
    kv[...] = kv_sums[...] * width
    key_mean = extra[0:1, :] * width
    scale = total * width / extra[2:3, :]

    def one(c, _):
        rows = pl.ds(pl.multiple_of(c * CHUNK, CHUNK), CHUNK)
        part = x[rows, :]
        query = jnp.dot(part, qw[...], preferred_element_type=F32)
        values = jnp.dot(part, vw[...], preferred_element_type=F32)
        feat = query * query * scale
        numer = jnp.dot(feat, kv[...], precision=HIGHEST, preferred_element_type=F32) + width * values
        denom = jnp.sum(feat * key_mean, 1, keepdims=True) + width
        graph = hop_zero[rows, :].astype(F32) + hop_one[rows, :].astype(F32)
        out[rows, :] = numer / denom + graph / 3.0
        return 0

    lax.fori_loop(0, x.shape[0] // CHUNK, one, 0)


def attention(total, x, qw, vw, kv_sums, extra, hop_zero, hop_one):
    rows = x.shape[0]
    return pl.pallas_call(
        functools.partial(attention_kernel, total),
        out_shape=pltpu.HBM((rows, D), F32),
        in_specs=[VMEM] * 7,
        out_specs=VMEM,
        scratch_shapes=[pltpu.VMEM((D, D), F32)],
        compiler_params=params(16),
        cost_estimate=cost(rows * D * D * 18, 6 << 20),
        name="attention",
    )(x, qw, vw, kv_sums, extra, hop_zero, hop_one)


def finish_kernel(first, rows, cols, count, tiles, blocks, part, base, gain, out, got, acc, mixing, done, sems, *lists):
    nblocks = part.shape[0] - 1
    loads = [
        pltpu.make_async_copy(blocks, got, sems.at[0]),
        pltpu.make_async_copy(part, acc, sems.at[1]),
        pltpu.make_async_copy(base, mixing, sems.at[2]),
    ]
    for load in loads:
        load.start()
    n = collect(rows, cols, count, first, first + blocks.shape[0], nblocks, lists)
    loads[0].wait()
    loads[1].wait()
    add_tiles(n, lists, tiles, got, acc)
    loads[2].wait()

    def one(b, _):
        mixed = mixing[b] + acc[b].astype(BF16).astype(F32) / 3.0
        center = mixed - jnp.mean(mixed, 1, keepdims=True)
        scale = lax.rsqrt(jnp.mean(center * center, 1, keepdims=True) + 1e-05)
        done[b] = (gain[...] * center * scale).astype(BF16)
        pltpu.make_async_copy(done.at[b], out.at[b], sems.at[3]).start()
        return 0

    lax.fori_loop(0, nblocks, one, 0)
    pltpu.make_async_copy(done, out, sems.at[3]).wait()


def finish(rows, cols, count, tiles, blocks, part, base, gain, first):
    nblocks = part.shape[0] - 1
    return pl.pallas_call(
        functools.partial(finish_kernel, first),
        out_shape=jax.ShapeDtypeStruct((nblocks, BLOCK, D), BF16),
        in_specs=[SMEM] * 3 + [VMEM, HBM, HBM, HBM, VMEM],
        out_specs=HBM,
        scratch_shapes=[
            pltpu.VMEM(blocks.shape, BF16),
            pltpu.VMEM(part.shape, F32),
            pltpu.VMEM(base.shape, F32),
            pltpu.VMEM((nblocks, BLOCK, D), BF16),
            pltpu.SemaphoreType.DMA((4,)),
        ] + lists_of(rows),
        compiler_params=params(24),
        name="halo_tiles_norm",
    )(rows, cols, count, tiles, in_hbm(blocks), in_hbm(part), in_hbm(base), gain)


def shards(x, qw, kw, vw, gw, gain, tiles, tile_rows, tile_cols, tile_count, send_list):
    rows_dev = x.shape[0]
    nblocks = rows_dev // BLOCK
    peers, groups = lax.axis_size("wide"), lax.axis_size("narrow")
    total = float(rows_dev * peers * groups)
    first = groups * nblocks
    slots = (tile_rows, tile_cols, tile_count, tiles)

    hop_zero, outgoing = start(send_list, x, gw, peers)
    received = lax.all_to_all(outgoing, "wide", 0, 0, tiled=True)
    group = lax.all_gather(hop_zero, "narrow", axis=0, tiled=True)
    mine = partial_sums(stats(x, qw, kw, vw, hop_zero))
    others = along_depth(mine)
    part = local_tiles(*slots, group, mine, nblocks)
    hop_one, outgoing = hop(send_list, *slots, received, part, others, first)
    received = lax.all_to_all(outgoing, "wide", 0, 0, tiled=True)
    group = lax.all_gather(hop_one, "narrow", axis=0, tiled=True)
    kv_sums, extra = whole_sums(mine, others)
    base = attention(
        total, x, qw, vw, kv_sums, extra, hop_zero.reshape(rows_dev, D), hop_one.reshape(rows_dev, D)
    )
    part = local_tiles(*slots, group, base, nblocks)
    out = finish(*slots, received, part, base.reshape(nblocks, BLOCK, D), gain[None, :], first)
    return out.reshape(rows_dev, D)


def solution(mesh):
    return jax.shard_map(
        shards,
        mesh=mesh,
        in_specs=(
            P(("wide", "narrow"), None),
            P(),
            P(),
            P(),
            P(),
            P(),
            P(("wide", "narrow"), None, None),
            P(("wide", "narrow"), None),
            P(("wide", "narrow"), None),
            P(("wide", "narrow")),
            P(("wide", "narrow"), None),
        ),
        out_specs=P(("wide", "narrow"), None),
        check_vma=False,
    )
```

```python
import functools

import jax
import jax.numpy as jnp
from jax import lax
from jax.experimental import pallas as pl
from jax.experimental.pallas import tpu as pltpu
from jax.sharding import PartitionSpec as P

D = 256
BLOCK = 128
UNROLL = 8
CHUNK = 256
NORM = 4
EXTRA = 8
CORE = ("wide", 0)
HALVE = (("wide", 4), ("wide", 5), ("narrow", 0), ("narrow", 1))
DEPTH = 8
JOIN = (("wide", 5), ("wide", 4), ("narrow", 1), ("narrow", 0))
F32 = jnp.float32
BF16 = jnp.bfloat16
HIGHEST = lax.Precision.HIGHEST
SMEM = pl.BlockSpec(memory_space=pltpu.SMEM)
VMEM = pl.BlockSpec(memory_space=pltpu.VMEM)
HBM = pl.BlockSpec(memory_space=pltpu.HBM)


def in_hbm(x):
    return pltpu.with_memory_space_constraint(x, pltpu.HBM)


def params(mib):
    return pltpu.CompilerParams(vmem_limit_bytes=mib << 20)


def cost(flops, nbytes):
    return pl.CostEstimate(flops=flops, bytes_accessed=nbytes, transcendentals=0)


def send_order(send, heads, nexts, zeros, out, sem):
    zeros[...] = jnp.zeros_like(zeros)

    def clear(b, _):
        heads[b] = -1
        return 0

    lax.fori_loop(0, heads.shape[0], clear, 0)

    def one(w, _):
        index = send[0, w]
        block = jnp.maximum(index, 0)

        @pl.when(index >= 0)
        def _():
            nexts[w] = heads[block]
            heads[block] = w

        @pl.when(index < 0)
        def _():
            pltpu.make_async_copy(zeros, out.at[w], sem).start()

        return 0

    lax.fori_loop(0, nexts.shape[0], one, 0)


def send_block(b, src, heads, nexts, h_out, out, sems):
    pltpu.make_async_copy(src.at[b], h_out.at[b], sems.at[0]).start()

    def one(w):
        pltpu.make_async_copy(src.at[b], out.at[w], sems.at[1]).start()
        return nexts[w]

    lax.while_loop(lambda w: w >= 0, one, heads[b])


def wait_sent(src, h_out, out, sems):
    pltpu.make_async_copy(src, h_out, sems.at[0]).wait()
    pltpu.make_async_copy(out, out, sems.at[1]).wait()


def send_scratch(nblocks, peers):
    return [
        pltpu.VMEM((nblocks, BLOCK, D), BF16),
        pltpu.VMEM((BLOCK, D), BF16),
        pltpu.SMEM((nblocks,), jnp.int32),
        pltpu.SMEM((peers,), jnp.int32),
        pltpu.SemaphoreType.DMA((2,)),
    ]


def start_kernel(send, x, weight, h_out, out, h_own, zeros, heads, nexts, sems, send_own, x_own, weight_own, loads):
    pieces = loads.shape[0] - 2
    rows = x.shape[0] // pieces
    per = rows // BLOCK
    sends = pltpu.make_async_copy(send, send_own, loads.at[0])
    weights = pltpu.make_async_copy(weight, weight_own, loads.at[1])
    sends.start()
    weights.start()
    parts = [
        pltpu.make_async_copy(x.at[pl.ds(p * rows, rows)], x_own.at[pl.ds(p * rows, rows)], loads.at[2 + p])
        for p in range(pieces)
    ]
    for part in parts:
        part.start()
    sends.wait()
    send_order(send_own, heads, nexts, zeros, out, sems.at[1])
    weights.wait()
    for p in range(pieces):
        parts[p].wait()
        for b in range(p * per, (p + 1) * per):
            h_own[b] = jnp.dot(
                x_own[b * BLOCK:(b + 1) * BLOCK, :], weight_own[...], preferred_element_type=F32
            ).astype(BF16)
        for b in range(p * per, (p + 1) * per):
            send_block(b, h_own, heads, nexts, h_out, out, sems)
    wait_sent(h_own, h_out, out, sems)


def start(send, x, weight, peers):
    nblocks = x.shape[0] // BLOCK
    pieces = 4
    return pl.pallas_call(
        start_kernel,
        out_shape=(pltpu.HBM((nblocks, BLOCK, D), BF16), pltpu.HBM((peers, BLOCK, D), BF16)),
        in_specs=[HBM] * 3,
        out_specs=(HBM, HBM),
        scratch_shapes=send_scratch(nblocks, peers) + [
            pltpu.SMEM(send.shape, jnp.int32),
            pltpu.VMEM(x.shape, BF16),
            pltpu.VMEM(weight.shape, BF16),
            pltpu.SemaphoreType.DMA((pieces + 2,)),
        ],
        compiler_params=params(16),
        name="project_send",
    )(in_hbm(send), in_hbm(x), in_hbm(weight))


def stats_kernel(x, qw, kw, vw, after, out, keys_sq, values, sums):
    steps = x.shape[0] // CHUNK

    def project(c, carry):
        ksum, qsum = carry
        rows = pl.ds(pl.multiple_of(c * CHUNK, CHUNK), CHUNK)
        part = x[rows, :]
        query = jnp.dot(part, qw[...], preferred_element_type=F32)
        keys = jnp.dot(part, kw[...], preferred_element_type=F32)
        values[rows, :] = jnp.dot(part, vw[...], preferred_element_type=F32)
        keys_sq[rows, :] = keys * keys
        ksum = ksum + jnp.sum(keys * keys, 0, keepdims=True)
        return ksum, qsum + jnp.sum(query * query, 0, keepdims=True)

    zero = jnp.zeros((1, D), F32)
    ksum, qsum = lax.fori_loop(0, steps, project, (zero, zero))
    ktotal = jnp.sum(ksum, 1, keepdims=True)
    qtotal = jnp.sum(qsum, 1, keepdims=True)
    divisor = jnp.where(ktotal > 0, ktotal, 1.0)
    sums[...] = jnp.zeros_like(sums)

    def one(c, _):
        rows = pl.ds(pl.multiple_of(c * CHUNK, CHUNK), CHUNK)
        feat = keys_sq[rows, :] / divisor
        sums[...] += lax.dot_general(
            feat, values[rows, :], (((0,), (0,)), ((), ())),
            precision=HIGHEST, preferred_element_type=F32,
        )
        return 0

    lax.fori_loop(0, steps, one, 0)
    row = lax.broadcasted_iota(jnp.int32, (EXTRA, D), 0)
    extra = jnp.where(row == 0, ksum / divisor, jnp.where(row == 1, ktotal, qtotal))
    out[0:D, :] = sums[...]
    out[D:, :] = extra


def bit_of(step):
    axis, bit = step
    return lax.axis_index(axis) >> bit & 1


def split(rows, extra, bit, keep, away):
    half = rows.shape[0] // 2
    keep[0:half, :] = rows[pl.ds(pl.multiple_of(bit * half, 8), half), :]
    away[0:half, :] = rows[pl.ds(pl.multiple_of((1 - bit) * half, 8), half), :]
    keep[half:half + EXTRA, :] = extra
    away[half:half + EXTRA, :] = extra


def stats(x, qw, kw, vw, after):
    rows = x.shape[0]
    return pl.pallas_call(
        stats_kernel,
        out_shape=jax.ShapeDtypeStruct((D + EXTRA, D), F32),
        in_specs=[VMEM] * 4 + [HBM],
        out_specs=VMEM,
        scratch_shapes=[pltpu.VMEM((rows, D), F32)] * 2 + [pltpu.VMEM((D, D), F32)],
        compiler_params=params(16),
        cost_estimate=cost(rows * D * D * 18, 2 << 20),
        name="attention_sums",
    )(x, qw, kw, vw, after)


def merged(parts):
    rows = parts[0].shape[0] - EXTRA
    extras = [p[rows:, :] for p in parts]
    added = functools.reduce(jnp.add, extras)
    total = added[1:2, :]
    weights = [e[1:2, :] / jnp.where(total > 0, total, 1.0) for e in extras]
    row = lax.broadcasted_iota(jnp.int32, (EXTRA, D), 0)
    extra = jnp.where(row == 0, functools.reduce(jnp.add, [e * w for e, w in zip(extras, weights)]), added)
    return functools.reduce(jnp.add, [p[0:rows, :] * w for p, w in zip(parts, weights)]), extra


def halve_kernel(step, mine, other, keep, away, scratch):
    sums, extra = merged((mine, other))
    scratch[...] = sums
    split(scratch, extra, bit_of(step), keep, away)


def halve(mine, other, step):
    rows = mine.shape[0] - EXTRA
    return pl.pallas_call(
        functools.partial(halve_kernel, step),
        out_shape=(jax.ShapeDtypeStruct((rows // 2 + EXTRA, D), F32),) * 2,
        in_specs=[VMEM, VMEM],
        out_specs=(VMEM, VMEM),
        scratch_shapes=[pltpu.VMEM((rows, D), F32)],
        name="halve_sums",
    )(mine, other)


def merge_kernel(core, *refs):
    out = refs[-1]
    parts = [ref[...] for ref in refs[:-1]]
    if core:
        parts[0] = jnp.where(bit_of(CORE) == 0, parts[0], 0.0)
    sums, extra = merged(parts)
    rows = sums.shape[0]
    out[0:rows, :] = sums
    out[rows:, :] = extra


def merge(*parts, core=False):
    return pl.pallas_call(
        functools.partial(merge_kernel, core),
        out_shape=jax.ShapeDtypeStruct(parts[0].shape, F32),
        in_specs=[VMEM] * len(parts),
        out_specs=VMEM,
        name="merge_sums",
    )(*parts)


def join_kernel(step, mine, other, out):
    rows = mine.shape[0]
    at = bit_of(step)
    out[pl.ds(pl.multiple_of(at * rows, 8), rows), :] = mine[...]
    out[pl.ds(pl.multiple_of((1 - at) * rows, 8), rows), :] = other[...]


def join(mine, other, step):
    return pl.pallas_call(
        functools.partial(join_kernel, step),
        out_shape=jax.ShapeDtypeStruct((2 * mine.shape[0], D), F32),
        in_specs=[VMEM, VMEM],
        out_specs=VMEM,
        name="join_sums",
    )(mine, other)


def swap(x, step):
    axis, bit = step
    return lax.ppermute(x, axis, [(i, i ^ 1 << bit) for i in range(lax.axis_size(axis))])


def partial_sums(mine):
    keep, away = halve(mine, swap(mine, CORE), HALVE[0])
    for done, step in zip(HALVE, HALVE[1:]):
        keep, away = halve(keep, swap(away, done), step)
    return merge(keep, swap(away, HALVE[-1]))


def along_depth(mine):
    span, reach = 2 * DEPTH, DEPTH // 2

    def shift(by):
        return [
            (i, i // span * span + (i + 2 * (by + reach * (i % 2))) % span)
            for i in range(lax.axis_size("wide"))
            if by + reach * (i % 2) < DEPTH
        ]

    return [lax.ppermute(mine, "wide", shift(by)) for by in range(1, reach + 1)]


def whole_sums(mine, others):
    mine = merge(mine, *others, core=True)
    mine = merge(mine, swap(mine, CORE))
    rows, extra = mine[:-EXTRA], mine[-EXTRA:]
    for step in JOIN:
        rows = join(rows, swap(rows, step), step)
    return rows, extra


def collect(rows, cols, count, first, last, spare, lists):
    slots, places, targets = lists

    def one(t, n):
        c = cols[0, t]
        slots[n] = t
        places[n] = c - first
        targets[n] = rows[0, t]
        return n + ((c >= first) & (c < last)).astype(jnp.int32)

    n = lax.fori_loop(0, count[0], one, jnp.int32(0))
    for u in range(UNROLL):
        slots[n + u] = 0
        places[n + u] = 0
        targets[n + u] = spare
    return n


def add_tiles(n, lists, tiles, blocks, acc):
    slots, places, targets = lists

    def step(i, _):
        prods = [
            jnp.dot(tiles[slots[i * UNROLL + u]], blocks[places[i * UNROLL + u]], preferred_element_type=F32)
            for u in range(UNROLL)
        ]
        for u in range(UNROLL):
            r = targets[i * UNROLL + u]
            acc[r] = acc[r] + prods[u]
        return 0

    lax.fori_loop(0, (n + UNROLL - 1) // UNROLL, step, 0)


def load_halo(n, places, blocks, got, sems):
    def one(i, _):
        for u in range(UNROLL):
            j = i * UNROLL + u
            pltpu.make_async_copy(blocks.at[places[j]], got.at[j], sems.at[i]).start()
        return 0

    lax.fori_loop(0, (n + UNROLL - 1) // UNROLL, one, 0)


def add_halo(n, lists, tiles, got, acc, sems):
    slots, places, targets = lists

    def step(i, _):
        at = pl.ds(i * UNROLL, UNROLL)
        pltpu.make_async_copy(got.at[at], got.at[at], sems.at[i]).wait()
        prods = [
            jnp.dot(tiles[slots[i * UNROLL + u]], got[i * UNROLL + u], preferred_element_type=F32)
            for u in range(UNROLL)
        ]
        for u in range(UNROLL):
            r = targets[i * UNROLL + u]
            acc[r] = acc[r] + prods[u]
        return 0

    lax.fori_loop(0, (n + UNROLL - 1) // UNROLL, step, 0)


def halo_scratch(rows, part):
    steps = -(-rows.shape[1] // UNROLL)
    return [
        pltpu.VMEM((steps * UNROLL, BLOCK, D), BF16),
        pltpu.VMEM(part.shape, F32),
        pltpu.VMEM(part.shape, F32),
        pltpu.SemaphoreType.DMA((steps + 1,)),
    ] + lists_of(rows)


def local_kernel(rows, cols, count, tiles, *refs):
    parts, after, acc, blocks, sems, lists = refs[:-7], refs[-7], refs[-6], refs[-5], refs[-4], refs[-3:]
    groups, nblocks = len(parts), parts[0].shape[0]
    me = lax.axis_index("narrow")
    loads = []
    for by, part in enumerate(parts):
        owner = lax.rem(me + groups - by, groups)
        place = blocks.at[pl.ds(owner * nblocks, nblocks)]
        loads.append(pltpu.make_async_copy(part, place, sems.at[by]))
        loads[-1].start()
    n = collect(rows, cols, count, 0, blocks.shape[0], nblocks, lists)
    acc[...] = jnp.zeros_like(acc)
    for load in loads:
        load.wait()
    add_tiles(n, lists, tiles, blocks, acc)


def lists_of(rows):
    return [pltpu.SMEM((rows.shape[1] + UNROLL,), jnp.int32)] * 3


def local_tiles(rows, cols, count, tiles, parts, after):
    nblocks = parts[0].shape[0]
    return pl.pallas_call(
        local_kernel,
        out_shape=pltpu.HBM((nblocks + 1, BLOCK, D), F32),
        in_specs=[SMEM, SMEM, SMEM, VMEM] + [HBM] * (len(parts) + 1),
        out_specs=VMEM,
        scratch_shapes=[
            pltpu.VMEM((len(parts) * nblocks, BLOCK, D), BF16),
            pltpu.SemaphoreType.DMA((len(parts),)),
        ] + lists_of(rows),
        compiler_params=params(16),
        cost_estimate=cost(48 * BLOCK * BLOCK * D * 2, 9 << 20),
        name="local_tiles",
    )(rows, cols, count, tiles, *map(in_hbm, parts), after)


def hop_kernel(first, send, rows, cols, count, tiles, blocks, part, *refs):
    h_out, out, got, acc, local, loads, *rest = refs[DEPTH // 2:]
    lists, (h_own, zeros, heads, nexts, sems) = rest[:3], rest[3:]
    nblocks = h_own.shape[0]
    n = collect(rows, cols, count, first, first + blocks.shape[0], nblocks, lists)
    load_halo(n, lists[1], blocks, got, loads)
    load = pltpu.make_async_copy(part, local, loads.at[loads.shape[0] - 1])
    load.start()
    send_order(send, heads, nexts, zeros, out, sems.at[1])
    acc[...] = jnp.zeros_like(acc)
    add_halo(n, lists, tiles, got, acc, loads)
    load.wait()

    def one(b, _):
        h_own[b] = (acc[b] + local[b]).astype(BF16)
        send_block(b, h_own, heads, nexts, h_out, out, sems)
        return 0

    lax.fori_loop(0, nblocks, one, 0)
    wait_sent(h_own, h_out, out, sems)


def hop(send, rows, cols, count, tiles, blocks, part, after, first):
    nblocks = part.shape[0] - 1
    return pl.pallas_call(
        functools.partial(hop_kernel, first),
        out_shape=(pltpu.HBM((nblocks, BLOCK, D), BF16), pltpu.HBM(blocks.shape, BF16)),
        in_specs=[SMEM] * 4 + [VMEM, HBM, HBM] + [HBM] * len(after),
        out_specs=(HBM, HBM),
        scratch_shapes=halo_scratch(rows, part) + send_scratch(nblocks, blocks.shape[0]),
        compiler_params=params(20),
        name="halo_tiles_send",
    )(send, rows, cols, count, tiles, in_hbm(blocks), in_hbm(part), *after)


def attention_kernel(total, x, qw, vw, kv_sums, extra, hop_zero, hop_one, out, kv):
    width = float(D)
    each = D >> len(HALVE)
    for place in range(1 << len(HALVE)):
        bits = {step: place >> at & 1 for at, step in enumerate(HALVE[::-1])}
        came = sum(bits[step] << at for at, step in enumerate(JOIN))
        kv[place * each:(place + 1) * each, :] = kv_sums[came * each:(came + 1) * each, :] * width
    key_mean = extra[0:1, :] * width
    scale = total * width / extra[2:3, :]

    def one(c, _):
        rows = pl.ds(pl.multiple_of(c * CHUNK, CHUNK), CHUNK)
        part = x[rows, :]
        query = jnp.dot(part, qw[...], preferred_element_type=F32)
        values = jnp.dot(part, vw[...], preferred_element_type=F32)
        feat = query * query * scale
        numer = jnp.dot(feat, kv[...], precision=HIGHEST, preferred_element_type=F32) + width * values
        denom = jnp.sum(feat * key_mean, 1, keepdims=True) + width
        graph = hop_zero[rows, :].astype(F32) + hop_one[rows, :].astype(F32)
        out[rows, :] = numer / denom + graph / 3.0
        return 0

    lax.fori_loop(0, x.shape[0] // CHUNK, one, 0)


def attention(total, x, qw, vw, kv_sums, extra, hop_zero, hop_one):
    rows = x.shape[0]
    return pl.pallas_call(
        functools.partial(attention_kernel, total),
        out_shape=pltpu.HBM((rows, D), F32),
        in_specs=[VMEM] * 7,
        out_specs=VMEM,
        scratch_shapes=[pltpu.VMEM((D, D), F32)],
        compiler_params=params(16),
        cost_estimate=cost(rows * D * D * 18, 6 << 20),
        name="attention",
    )(x, qw, vw, kv_sums, extra, hop_zero, hop_one)


def finish_kernel(first, rows, cols, count, tiles, blocks, part, base, gain, out, got, acc, local, loads, *rest):
    lists, (mixing, base_sem, done, sem) = rest[:3], rest[3:]
    nblocks = part.shape[0] - 1
    n = collect(rows, cols, count, first, first + blocks.shape[0], nblocks, lists)
    load_halo(n, lists[1], blocks, got, loads)
    late = [
        pltpu.make_async_copy(part, local, loads.at[loads.shape[0] - 1]),
        pltpu.make_async_copy(base, mixing, base_sem),
    ]
    for load in late:
        load.start()
    acc[...] = jnp.zeros_like(acc)
    add_halo(n, lists, tiles, got, acc, loads)
    for load in late:
        load.wait()

    def some(i, _):
        for u in range(NORM):
            b = i * NORM + u
            mixed = mixing[b] + (acc[b] + local[b]).astype(BF16).astype(F32) / 3.0
            center = mixed - jnp.mean(mixed, 1, keepdims=True)
            scale = lax.rsqrt(jnp.mean(center * center, 1, keepdims=True) + 1e-05)
            done[b] = (gain[...] * center * scale).astype(BF16)
        at = pl.ds(i * NORM, NORM)
        pltpu.make_async_copy(done.at[at], out.at[at], sem).start()
        return 0

    lax.fori_loop(0, nblocks // NORM, some, 0)
    pltpu.make_async_copy(done, out, sem).wait()


def finish(rows, cols, count, tiles, blocks, part, base, gain, first):
    nblocks = part.shape[0] - 1
    return pl.pallas_call(
        functools.partial(finish_kernel, first),
        out_shape=jax.ShapeDtypeStruct((nblocks, BLOCK, D), BF16),
        in_specs=[SMEM] * 3 + [VMEM, HBM, HBM, HBM, VMEM],
        out_specs=HBM,
        scratch_shapes=halo_scratch(rows, part) + [
            pltpu.VMEM(base.shape, F32), pltpu.SemaphoreType.DMA,
            pltpu.VMEM((nblocks, BLOCK, D), BF16), pltpu.SemaphoreType.DMA,
        ],
        compiler_params=params(20),
        name="halo_tiles_norm",
    )(rows, cols, count, tiles, in_hbm(blocks), in_hbm(part), in_hbm(base), gain)


def group_blocks(own):
    groups = lax.axis_size("narrow")
    return [own] + [
        lax.ppermute(own, "narrow", [(i, (i + by) % groups) for i in range(groups)])
        for by in range(1, groups)
    ]


def shards(x, qw, kw, vw, gw, gain, tiles, tile_rows, tile_cols, tile_count, send_list):
    rows_dev = x.shape[0]
    nblocks = rows_dev // BLOCK
    peers, groups = lax.axis_size("wide"), lax.axis_size("narrow")
    total = float(rows_dev * peers * groups)
    first = groups * nblocks
    slots = (tile_rows, tile_cols, tile_count, tiles)

    hop_zero, outgoing = start(send_list, x, gw, peers)
    received = lax.all_to_all(outgoing, "wide", 0, 0, tiled=True)
    group = group_blocks(hop_zero)
    mine = partial_sums(stats(x, qw, kw, vw, hop_zero))
    others = along_depth(mine)
    part = local_tiles(*slots, group, mine)
    hop_one, outgoing = hop(send_list, *slots, received, part, others, first)
    received = lax.all_to_all(outgoing, "wide", 0, 0, tiled=True)
    group = group_blocks(hop_one)
    kv_sums, extra = whole_sums(mine, others)
    base = attention(
        total, x, qw, vw, kv_sums, extra, hop_zero.reshape(rows_dev, D), hop_one.reshape(rows_dev, D)
    )
    part = local_tiles(*slots, group, base)
    out = finish(*slots, received, part, base.reshape(nblocks, BLOCK, D), gain[None, :], first)
    return out.reshape(rows_dev, D)


def solution(mesh):
    return jax.shard_map(
        shards,
        mesh=mesh,
        in_specs=(
            P(("wide", "narrow"), None),
            P(),
            P(),
            P(),
            P(),
            P(),
            P(("wide", "narrow"), None, None),
            P(("wide", "narrow"), None),
            P(("wide", "narrow"), None),
            P(("wide", "narrow")),
            P(("wide", "narrow"), None),
        ),
        out_specs=P(("wide", "narrow"), None),
        check_vma=False,
    )
```

```python
import functools

import jax
import jax.numpy as jnp
from jax import lax
from jax.experimental import pallas as pl
from jax.experimental.pallas import tpu as pltpu
from jax.sharding import PartitionSpec as P

D = 256
BLOCK = 128
PAIRS = 4
CHUNK = 256
NORM = 4
EXTRA = 8
CORE = ("wide", 0)
HALVE = (("wide", 4), ("wide", 5), ("narrow", 0), ("narrow", 1))
DEPTH = 8
AROUND = ((2, 4), (6, 3), (1, 5), (7, 0))
JOIN = (("wide", 5), ("wide", 4), ("narrow", 1), ("narrow", 0))
F32 = jnp.float32
BF16 = jnp.bfloat16
HIGHEST = lax.Precision.HIGHEST
SMEM = pl.BlockSpec(memory_space=pltpu.SMEM)
VMEM = pl.BlockSpec(memory_space=pltpu.VMEM)
HBM = pl.BlockSpec(memory_space=pltpu.HBM)


def in_hbm(x):
    return pltpu.with_memory_space_constraint(x, pltpu.HBM)


def params(mib):
    return pltpu.CompilerParams(vmem_limit_bytes=mib << 20)


def cost(flops, nbytes):
    return pl.CostEstimate(flops=flops, bytes_accessed=nbytes, transcendentals=0)


def send_order(send, heads, nexts, zeros, out, sem):
    zeros[...] = jnp.zeros_like(zeros)

    def clear(b, _):
        heads[b] = -1
        return 0

    lax.fori_loop(0, heads.shape[0], clear, 0)

    def one(w, _):
        index = send[0, w]
        block = jnp.maximum(index, 0)

        @pl.when(index >= 0)
        def _():
            nexts[w] = heads[block]
            heads[block] = w

        @pl.when(index < 0)
        def _():
            pltpu.make_async_copy(zeros, out.at[w], sem).start()

        return 0

    lax.fori_loop(0, nexts.shape[0], one, 0)


def send_block(b, src, heads, nexts, h_out, out, sems):
    pltpu.make_async_copy(src.at[b], h_out.at[b], sems.at[0]).start()

    def one(w):
        pltpu.make_async_copy(src.at[b], out.at[w], sems.at[1]).start()
        return nexts[w]

    lax.while_loop(lambda w: w >= 0, one, heads[b])


def wait_sent(src, h_out, out, sems):
    pltpu.make_async_copy(src, h_out, sems.at[0]).wait()
    pltpu.make_async_copy(out, out, sems.at[1]).wait()


def send_scratch(nblocks, peers):
    return [
        pltpu.VMEM((nblocks, BLOCK, D), BF16),
        pltpu.VMEM((BLOCK, D), BF16),
        pltpu.SMEM((nblocks,), jnp.int32),
        pltpu.SMEM((peers,), jnp.int32),
        pltpu.SemaphoreType.DMA((2,)),
    ]


def start_kernel(send, x, weight, h_out, out, h_own, zeros, heads, nexts, sems, send_own, x_own, weight_own, loads):
    pieces = loads.shape[0] - 2
    rows = x.shape[0] // pieces
    per = rows // BLOCK
    sends = pltpu.make_async_copy(send, send_own, loads.at[0])
    weights = pltpu.make_async_copy(weight, weight_own, loads.at[1])
    sends.start()
    weights.start()
    parts = [
        pltpu.make_async_copy(x.at[pl.ds(p * rows, rows)], x_own.at[pl.ds(p * rows, rows)], loads.at[2 + p])
        for p in range(pieces)
    ]
    for part in parts:
        part.start()
    sends.wait()
    send_order(send_own, heads, nexts, zeros, out, sems.at[1])
    weights.wait()
    for p in range(pieces):
        parts[p].wait()
        for b in range(p * per, (p + 1) * per):
            h_own[b] = jnp.dot(
                x_own[b * BLOCK:(b + 1) * BLOCK, :], weight_own[...], preferred_element_type=F32
            ).astype(BF16)
        for b in range(p * per, (p + 1) * per):
            send_block(b, h_own, heads, nexts, h_out, out, sems)
    wait_sent(h_own, h_out, out, sems)


def start(send, x, weight, peers):
    nblocks = x.shape[0] // BLOCK
    pieces = 4
    return pl.pallas_call(
        start_kernel,
        out_shape=(pltpu.HBM((nblocks, BLOCK, D), BF16), pltpu.HBM((peers, BLOCK, D), BF16)),
        in_specs=[HBM] * 3,
        out_specs=(HBM, HBM),
        scratch_shapes=send_scratch(nblocks, peers) + [
            pltpu.SMEM(send.shape, jnp.int32),
            pltpu.VMEM(x.shape, BF16),
            pltpu.VMEM(weight.shape, BF16),
            pltpu.SemaphoreType.DMA((pieces + 2,)),
        ],
        compiler_params=params(16),
        name="project_send",
    )(in_hbm(send), in_hbm(x), in_hbm(weight))


def stats_kernel(x, qw, kw, vw, after, out, keys_sq, values, sums):
    steps = x.shape[0] // CHUNK

    def project(c, carry):
        ksum, qsum = carry
        rows = pl.ds(pl.multiple_of(c * CHUNK, CHUNK), CHUNK)
        part = x[rows, :]
        query = jnp.dot(part, qw[...], preferred_element_type=F32)
        keys = jnp.dot(part, kw[...], preferred_element_type=F32)
        values[rows, :] = jnp.dot(part, vw[...], preferred_element_type=F32)
        keys_sq[rows, :] = keys * keys
        ksum = ksum + jnp.sum(keys * keys, 0, keepdims=True)
        return ksum, qsum + jnp.sum(query * query, 0, keepdims=True)

    zero = jnp.zeros((1, D), F32)
    ksum, qsum = lax.fori_loop(0, steps, project, (zero, zero))
    ktotal = jnp.sum(ksum, 1, keepdims=True)
    qtotal = jnp.sum(qsum, 1, keepdims=True)
    divisor = jnp.where(ktotal > 0, ktotal, 1.0)
    sums[...] = jnp.zeros_like(sums)

    def one(c, _):
        rows = pl.ds(pl.multiple_of(c * CHUNK, CHUNK), CHUNK)
        feat = keys_sq[rows, :] / divisor
        sums[...] += lax.dot_general(
            feat, values[rows, :], (((0,), (0,)), ((), ())),
            precision=HIGHEST, preferred_element_type=F32,
        )
        return 0

    lax.fori_loop(0, steps, one, 0)
    row = lax.broadcasted_iota(jnp.int32, (EXTRA, D), 0)
    extra = jnp.where(row == 0, ksum / divisor, jnp.where(row == 1, ktotal, qtotal))
    out[0:D, :] = sums[...]
    out[D:, :] = extra


def bit_of(step):
    axis, bit = step
    return lax.axis_index(axis) >> bit & 1


def split(rows, extra, bit, keep, away):
    half = rows.shape[0] // 2
    keep[0:half, :] = rows[pl.ds(pl.multiple_of(bit * half, 8), half), :]
    away[0:half, :] = rows[pl.ds(pl.multiple_of((1 - bit) * half, 8), half), :]
    keep[half:half + EXTRA, :] = extra
    away[half:half + EXTRA, :] = extra


def stats(x, qw, kw, vw, after):
    rows = x.shape[0]
    return pl.pallas_call(
        stats_kernel,
        out_shape=jax.ShapeDtypeStruct((D + EXTRA, D), F32),
        in_specs=[VMEM] * 4 + [HBM],
        out_specs=VMEM,
        scratch_shapes=[pltpu.VMEM((rows, D), F32)] * 2 + [pltpu.VMEM((D, D), F32)],
        compiler_params=params(16),
        cost_estimate=cost(rows * D * D * 18, 2 << 20),
        name="attention_sums",
    )(x, qw, kw, vw, after)


def merged(parts):
    rows = parts[0].shape[0] - EXTRA
    extras = [p[rows:, :] for p in parts]
    added = functools.reduce(jnp.add, extras)
    total = added[1:2, :]
    weights = [e[1:2, :] / jnp.where(total > 0, total, 1.0) for e in extras]
    row = lax.broadcasted_iota(jnp.int32, (EXTRA, D), 0)
    extra = jnp.where(row == 0, functools.reduce(jnp.add, [e * w for e, w in zip(extras, weights)]), added)
    return functools.reduce(jnp.add, [p[0:rows, :] * w for p, w in zip(parts, weights)]), extra


def halve_kernel(step, mine, other, keep, away, scratch):
    sums, extra = merged((mine, other))
    scratch[...] = sums
    split(scratch, extra, bit_of(step), keep, away)


def halve(mine, other, step):
    rows = mine.shape[0] - EXTRA
    return pl.pallas_call(
        functools.partial(halve_kernel, step),
        out_shape=(jax.ShapeDtypeStruct((rows // 2 + EXTRA, D), F32),) * 2,
        in_specs=[VMEM, VMEM],
        out_specs=(VMEM, VMEM),
        scratch_shapes=[pltpu.VMEM((rows, D), F32)],
        name="halve_sums",
    )(mine, other)


def merge_kernel(core, *refs):
    out = refs[-1]
    parts = [ref[...] for ref in refs[:-1]]
    if core:
        parts[0] = jnp.where(bit_of(CORE) == 0, parts[0], 0.0)
    sums, extra = merged(parts)
    rows = sums.shape[0]
    out[0:rows, :] = sums
    out[rows:, :] = extra


def merge(*parts, core=False):
    return pl.pallas_call(
        functools.partial(merge_kernel, core),
        out_shape=jax.ShapeDtypeStruct(parts[0].shape, F32),
        in_specs=[VMEM] * len(parts),
        out_specs=VMEM,
        name="merge_sums",
    )(*parts)


def join_kernel(step, mine, other, out):
    rows = mine.shape[0]
    at = bit_of(step)
    out[pl.ds(pl.multiple_of(at * rows, 8), rows), :] = mine[...]
    out[pl.ds(pl.multiple_of((1 - at) * rows, 8), rows), :] = other[...]


def join(mine, other, step):
    return pl.pallas_call(
        functools.partial(join_kernel, step),
        out_shape=jax.ShapeDtypeStruct((2 * mine.shape[0], D), F32),
        in_specs=[VMEM, VMEM],
        out_specs=VMEM,
        name="join_sums",
    )(mine, other)


def swap(x, step):
    axis, bit = step
    return lax.ppermute(x, axis, [(i, i ^ 1 << bit) for i in range(lax.axis_size(axis))])


def partial_sums(mine):
    keep, away = halve(mine, swap(mine, CORE), HALVE[0])
    for done, step in zip(HALVE, HALVE[1:]):
        keep, away = halve(keep, swap(away, done), step)
    return merge(keep, swap(away, HALVE[-1]))


def along_depth(mine):
    span = 2 * DEPTH

    def shift(by):
        return [
            (i, i // span * span + (i + 2 * by[i % 2]) % span)
            for i in range(lax.axis_size("wide"))
            if by[i % 2]
        ]

    return [lax.ppermute(mine, "wide", shift(by)) for by in AROUND]


def whole_sums(mine, others):
    mine = merge(mine, *others, core=True)
    mine = merge(mine, swap(mine, CORE))
    rows, extra = mine[:-EXTRA], mine[-EXTRA:]
    for step in JOIN:
        rows = join(rows, swap(rows, step), step)
    return rows, extra


def plan_kernel(nblocks, first, last, rows, cols, count, local, halo, heads, nexts):
    for out, low, high in ((local, 0, first), (halo, first, last)):
        def clear(r, _):
            heads[r] = -1
            return 0

        lax.fori_loop(0, nblocks, clear, 0)

        def one(t, _):
            c, r = cols[0, t], rows[0, t]

            @pl.when((c >= low) & (c < high))
            def _():
                nexts[t] = heads[r]
                heads[r] = t

            return 0

        lax.fori_loop(0, count[0], one, 0)

        def place(r, n):
            def pair(at):
                t, n = at
                other = nexts[t]
                both = other >= 0
                second = jnp.where(both, other, t)
                out[0, n] = t
                out[1, n] = second
                out[2, n] = cols[0, t] - low
                out[3, n] = cols[0, second] - low
                out[4, n] = both.astype(jnp.int32)
                out[5, n] = r
                return jnp.where(both, nexts[second], -1), n + 1

            return lax.while_loop(lambda at: at[0] >= 0, pair, (heads[r], n))[1]

        n = lax.fori_loop(0, nblocks, place, jnp.int32(0))
        for u in range(PAIRS):
            for line in range(5):
                out[line, n + u] = 0
            out[5, n + u] = nblocks
        out[6, 0] = (n + PAIRS - 1) // PAIRS


def plan(rows, cols, count, nblocks, first, last, after):
    slots = rows.shape[1]
    width = -(-((slots + nblocks) // 2 + PAIRS) // PAIRS) * PAIRS
    shape = jax.ShapeDtypeStruct((8, width), jnp.int32)

    def kernel(rows, cols, count, after, *refs):
        plan_kernel(nblocks, first, last, rows, cols, count, *refs)

    return pl.pallas_call(
        kernel,
        out_shape=(shape, shape),
        in_specs=[SMEM] * 3 + [HBM],
        out_specs=(SMEM, SMEM),
        scratch_shapes=[pltpu.SMEM((nblocks,), jnp.int32), pltpu.SMEM((slots,), jnp.int32)],
        name="plan_tiles",
    )(rows, cols, count, after)


def add_pairs(steps, tiles, two_blocks, acc, before):
    def step(i, _):
        before(i)
        prods = []
        for u in range(PAIRS):
            j = i * PAIRS + u
            second = tiles[steps[1, j]]
            second = jnp.where(steps[4, j] > 0, second, jnp.zeros_like(second))
            both = jnp.concatenate([tiles[steps[0, j]], second], 1)
            prods.append(jnp.dot(both, two_blocks(j), preferred_element_type=F32))
        for u in range(PAIRS):
            r = steps[5, i * PAIRS + u]
            acc[r] = acc[r] + prods[u]
        return 0

    lax.fori_loop(0, steps[6, 0], step, 0)


def local_kernel(nparts, steps, tiles, *refs):
    parts, (base, out, blocks, acc, result, sems) = refs[:nparts], refs[nparts:]
    nblocks = parts[0].shape[0]
    me = lax.axis_index("narrow")
    loads = []
    for by, part in enumerate(parts):
        owner = lax.rem(me + nparts - by, nparts)
        place = blocks.at[pl.ds(owner * nblocks, nblocks)]
        loads.append(pltpu.make_async_copy(part, place, sems.at[by]))
    with_base = base.shape == result.shape
    if with_base:
        loads.append(pltpu.make_async_copy(base, result, sems.at[nparts]))
    for load in loads:
        load.start()
    acc[...] = jnp.zeros_like(acc)
    for load in loads:
        load.wait()
    add_pairs(
        steps, tiles, lambda j: jnp.concatenate([blocks[steps[2, j]], blocks[steps[3, j]]], 0), acc, lambda i: None
    )
    if with_base:
        result[...] = result[...] + acc[:nblocks] / 3.0
    else:
        result[...] = acc[:nblocks]
    store = pltpu.make_async_copy(result, out, sems.at[nparts + 1])
    store.start()
    store.wait()


def local_tiles(steps, tiles, parts, base):
    nblocks = parts[0].shape[0]
    return pl.pallas_call(
        functools.partial(local_kernel, len(parts)),
        out_shape=pltpu.HBM((nblocks, BLOCK, D), F32),
        in_specs=[SMEM, VMEM] + [HBM] * (len(parts) + 1),
        out_specs=HBM,
        scratch_shapes=[
            pltpu.VMEM((len(parts) * nblocks, BLOCK, D), BF16),
            pltpu.VMEM((nblocks + 1, BLOCK, D), F32),
            pltpu.VMEM((nblocks, BLOCK, D), F32),
            pltpu.SemaphoreType.DMA((len(parts) + 2,)),
        ],
        compiler_params=params(20),
        cost_estimate=cost(48 * BLOCK * BLOCK * D * 2, 9 << 20),
        name="local_tiles",
    )(steps, tiles, *map(in_hbm, parts), in_hbm(base))


def load_halo(steps, blocks, got, sems):
    def one(i, _):
        for u in range(PAIRS):
            j = i * PAIRS + u
            for half in range(2):
                place = got.at[j, pl.ds(half * BLOCK, BLOCK)]
                pltpu.make_async_copy(blocks.at[steps[2 + half, j]], place, sems.at[i]).start()
        return 0

    lax.fori_loop(0, steps[6, 0], one, 0)


def add_halo(steps, tiles, got, acc, sems):
    def before(i):
        at = pl.ds(i * PAIRS, PAIRS)
        pltpu.make_async_copy(got.at[at], got.at[at], sems.at[i]).wait()

    add_pairs(steps, tiles, lambda j: got[j], acc, before)


def halo_scratch(steps, part):
    nblocks = part.shape[0]
    return [
        pltpu.VMEM((steps.shape[1], 2 * BLOCK, D), BF16),
        pltpu.VMEM((nblocks + 1, BLOCK, D), F32),
        pltpu.VMEM(part.shape, F32),
        pltpu.SemaphoreType.DMA((steps.shape[1] // PAIRS + 1,)),
    ]


def hop_kernel(send, steps, tiles, blocks, part, *refs):
    h_out, out, got, acc, local, loads, h_own, zeros, heads, nexts, sems = refs[len(AROUND):]
    nblocks = h_own.shape[0]
    load_halo(steps, blocks, got, loads)
    load = pltpu.make_async_copy(part, local, loads.at[loads.shape[0] - 1])
    load.start()
    send_order(send, heads, nexts, zeros, out, sems.at[1])
    acc[...] = jnp.zeros_like(acc)
    add_halo(steps, tiles, got, acc, loads)
    load.wait()

    def one(b, _):
        h_own[b] = (acc[b] + local[b]).astype(BF16)
        send_block(b, h_own, heads, nexts, h_out, out, sems)
        return 0

    lax.fori_loop(0, nblocks, one, 0)
    wait_sent(h_own, h_out, out, sems)


def hop(send, steps, tiles, blocks, part, after):
    nblocks = part.shape[0]
    return pl.pallas_call(
        hop_kernel,
        out_shape=(pltpu.HBM((nblocks, BLOCK, D), BF16), pltpu.HBM(blocks.shape, BF16)),
        in_specs=[SMEM, SMEM, VMEM, HBM, HBM] + [HBM] * len(after),
        out_specs=(HBM, HBM),
        scratch_shapes=halo_scratch(steps, part) + send_scratch(nblocks, blocks.shape[0]),
        compiler_params=params(20),
        name="halo_tiles_send",
    )(send, steps, tiles, in_hbm(blocks), in_hbm(part), *after)


def attention_kernel(total, x, qw, vw, kv_sums, extra, hop_zero, hop_one, out, kv):
    width = float(D)
    each = D >> len(HALVE)
    for place in range(1 << len(HALVE)):
        bits = {step: place >> at & 1 for at, step in enumerate(HALVE[::-1])}
        came = sum(bits[step] << at for at, step in enumerate(JOIN))
        kv[place * each:(place + 1) * each, :] = kv_sums[came * each:(came + 1) * each, :] * width
    key_mean = extra[0:1, :] * width
    scale = total * width / extra[2:3, :]

    def one(c, _):
        rows = pl.ds(pl.multiple_of(c * CHUNK, CHUNK), CHUNK)
        part = x[rows, :]
        query = jnp.dot(part, qw[...], preferred_element_type=F32)
        values = jnp.dot(part, vw[...], preferred_element_type=F32)
        feat = query * query * scale
        numer = jnp.dot(feat, kv[...], precision=HIGHEST, preferred_element_type=F32) + width * values
        denom = jnp.sum(feat * key_mean, 1, keepdims=True) + width
        graph = hop_zero[rows, :].astype(F32) + hop_one[rows, :].astype(F32)
        out[rows, :] = numer / denom + graph / 3.0
        return 0

    lax.fori_loop(0, x.shape[0] // CHUNK, one, 0)


def attention(total, x, qw, vw, kv_sums, extra, hop_zero, hop_one):
    rows = x.shape[0]
    return pl.pallas_call(
        functools.partial(attention_kernel, total),
        out_shape=pltpu.HBM((rows, D), F32),
        in_specs=[VMEM] * 7,
        out_specs=VMEM,
        scratch_shapes=[pltpu.VMEM((D, D), F32)],
        compiler_params=params(16),
        cost_estimate=cost(rows * D * D * 18, 6 << 20),
        name="attention",
    )(x, qw, vw, kv_sums, extra, hop_zero, hop_one)


def finish_kernel(steps, tiles, blocks, base, gain, out, got, acc, mixing, loads, done, sem):
    nblocks = base.shape[0]
    load_halo(steps, blocks, got, loads)
    load = pltpu.make_async_copy(base, mixing, loads.at[loads.shape[0] - 1])
    load.start()
    acc[...] = jnp.zeros_like(acc)
    add_halo(steps, tiles, got, acc, loads)
    load.wait()

    def some(i, _):
        for u in range(NORM):
            b = i * NORM + u
            mixed = mixing[b] + acc[b] / 3.0
            center = mixed - jnp.mean(mixed, 1, keepdims=True)
            scale = lax.rsqrt(jnp.mean(center * center, 1, keepdims=True) + 1e-05)
            done[b] = (gain[...] * center * scale).astype(BF16)
        at = pl.ds(i * NORM, NORM)
        pltpu.make_async_copy(done.at[at], out.at[at], sem).start()
        return 0

    lax.fori_loop(0, nblocks // NORM, some, 0)
    pltpu.make_async_copy(done, out, sem).wait()


def finish(steps, tiles, blocks, base, gain):
    nblocks = base.shape[0]
    return pl.pallas_call(
        finish_kernel,
        out_shape=jax.ShapeDtypeStruct((nblocks, BLOCK, D), BF16),
        in_specs=[SMEM, VMEM, HBM, HBM, VMEM],
        out_specs=HBM,
        scratch_shapes=halo_scratch(steps, base) + [
            pltpu.VMEM((nblocks, BLOCK, D), BF16), pltpu.SemaphoreType.DMA,
        ],
        compiler_params=params(20),
        name="halo_tiles_norm",
    )(steps, tiles, in_hbm(blocks), in_hbm(base), gain)


def group_blocks(own):
    groups = lax.axis_size("narrow")
    return [own] + [
        lax.ppermute(own, "narrow", [(i, (i + by) % groups) for i in range(groups)])
        for by in range(1, groups)
    ]


def shards(x, qw, kw, vw, gw, gain, tiles, tile_rows, tile_cols, tile_count, send_list):
    rows_dev = x.shape[0]
    nblocks = rows_dev // BLOCK
    peers, groups = lax.axis_size("wide"), lax.axis_size("narrow")
    total = float(rows_dev * peers * groups)
    first = groups * nblocks

    hop_zero, outgoing = start(send_list, x, gw, peers)
    received = lax.all_to_all(outgoing, "wide", 0, 0, tiled=True)
    group = group_blocks(hop_zero)
    mine = partial_sums(stats(x, qw, kw, vw, hop_zero))
    others = along_depth(mine)
    local, halo = plan(tile_rows, tile_cols, tile_count, nblocks, first, first + peers, hop_zero)
    part = local_tiles(local, tiles, group, mine)
    hop_one, outgoing = hop(send_list, halo, tiles, received, part, others)
    received = lax.all_to_all(outgoing, "wide", 0, 0, tiled=True)
    group = group_blocks(hop_one)
    kv_sums, extra = whole_sums(mine, others)
    base = attention(
        total, x, qw, vw, kv_sums, extra, hop_zero.reshape(rows_dev, D), hop_one.reshape(rows_dev, D)
    )
    base = local_tiles(local, tiles, group, base.reshape(nblocks, BLOCK, D))
    out = finish(halo, tiles, received, base, gain[None, :])
    return out.reshape(rows_dev, D)


def solution(mesh):
    return jax.shard_map(
        shards,
        mesh=mesh,
        in_specs=(
            P(("wide", "narrow"), None),
            P(),
            P(),
            P(),
            P(),
            P(),
            P(("wide", "narrow"), None, None),
            P(("wide", "narrow"), None),
            P(("wide", "narrow"), None),
            P(("wide", "narrow")),
            P(("wide", "narrow"), None),
        ),
        out_specs=P(("wide", "narrow"), None),
        check_vma=False,
    )
```

```python
import functools

import jax
import jax.numpy as jnp
from jax import lax
from jax.experimental import pallas as pl
from jax.experimental.pallas import tpu as pltpu
from jax.sharding import PartitionSpec as P

D = 256
BLOCK = 128
PAIRS = 4
CHUNK = 256
NORM = 4
EXTRA = 8
CORE = ("wide", 0)
HALVE = (("wide", 4), ("wide", 5), ("narrow", 0), ("narrow", 1))
DEPTH = 8
AROUND = ((2, 4), (6, 3), (1, 5), (7, 0))
JOIN = (("wide", 5), ("wide", 4), ("narrow", 1), ("narrow", 0))
F32 = jnp.float32
BF16 = jnp.bfloat16
HIGHEST = lax.Precision.HIGHEST
SMEM = pl.BlockSpec(memory_space=pltpu.SMEM)
VMEM = pl.BlockSpec(memory_space=pltpu.VMEM)
HBM = pl.BlockSpec(memory_space=pltpu.HBM)


def in_hbm(x):
    return pltpu.with_memory_space_constraint(x, pltpu.HBM)


def params(mib):
    return pltpu.CompilerParams(vmem_limit_bytes=mib << 20)


def cost(flops, nbytes):
    return pl.CostEstimate(flops=flops, bytes_accessed=nbytes, transcendentals=0)


def send_order(send, heads, nexts, zeros, out, sem):
    zeros[...] = jnp.zeros_like(zeros)

    def clear(b, _):
        heads[b] = -1
        return 0

    lax.fori_loop(0, heads.shape[0], clear, 0)

    def one(w, _):
        index = send[0, w]
        block = jnp.maximum(index, 0)

        @pl.when(index >= 0)
        def _():
            nexts[w] = heads[block]
            heads[block] = w

        @pl.when(index < 0)
        def _():
            pltpu.make_async_copy(zeros, out.at[w], sem).start()

        return 0

    lax.fori_loop(0, nexts.shape[0], one, 0)


def send_block(b, src, heads, nexts, h_out, out, sems):
    if h_out is not None:
        pltpu.make_async_copy(src.at[b], h_out.at[b], sems.at[0]).start()

    def one(w):
        pltpu.make_async_copy(src.at[b], out.at[w], sems.at[1]).start()
        return nexts[w]

    lax.while_loop(lambda w: w >= 0, one, heads[b])


def wait_sent(src, h_out, out, sems):
    if h_out is not None:
        pltpu.make_async_copy(src, h_out, sems.at[0]).wait()
    pltpu.make_async_copy(out, out, sems.at[1]).wait()


def send_scratch(nblocks, peers):
    return [
        pltpu.VMEM((nblocks, BLOCK, D), BF16),
        pltpu.VMEM((BLOCK, D), BF16),
        pltpu.SMEM((nblocks,), jnp.int32),
        pltpu.SMEM((peers,), jnp.int32),
        pltpu.SemaphoreType.DMA((2,)),
    ]


def start_kernel(send, x, weight, out, h_own, zeros, heads, nexts, sems, send_own, x_own, weight_own, loads):
    pieces = loads.shape[0] - 2
    rows = x.shape[0] // pieces
    per = rows // BLOCK
    sends = pltpu.make_async_copy(send, send_own, loads.at[0])
    weights = pltpu.make_async_copy(weight, weight_own, loads.at[1])
    sends.start()
    weights.start()
    parts = [
        pltpu.make_async_copy(x.at[pl.ds(p * rows, rows)], x_own.at[pl.ds(p * rows, rows)], loads.at[2 + p])
        for p in range(pieces)
    ]
    for part in parts:
        part.start()
    sends.wait()
    send_order(send_own, heads, nexts, zeros, out, sems.at[1])
    weights.wait()
    for p in range(pieces):
        parts[p].wait()
        for b in range(p * per, (p + 1) * per):
            h_own[b] = jnp.dot(
                x_own[b * BLOCK:(b + 1) * BLOCK, :], weight_own[...], preferred_element_type=F32
            ).astype(BF16)
        for b in range(p * per, (p + 1) * per):
            send_block(b, h_own, heads, nexts, None, out, sems)
    wait_sent(h_own, None, out, sems)


def start(send, x, weight, peers):
    nblocks = x.shape[0] // BLOCK
    pieces = 4
    return pl.pallas_call(
        start_kernel,
        out_shape=pltpu.HBM((peers, BLOCK, D), BF16),
        in_specs=[HBM] * 3,
        out_specs=HBM,
        scratch_shapes=send_scratch(nblocks, peers) + [
            pltpu.SMEM(send.shape, jnp.int32),
            pltpu.VMEM(x.shape, BF16),
            pltpu.VMEM(weight.shape, BF16),
            pltpu.SemaphoreType.DMA((pieces + 2,)),
        ],
        compiler_params=params(16),
        name="project_send",
    )(in_hbm(send), in_hbm(x), in_hbm(weight))


def own_kernel(x, weight, after, out):
    def one(b, _):
        rows = pl.ds(pl.multiple_of(b * BLOCK, BLOCK), BLOCK)
        out[b] = jnp.dot(x[rows, :], weight[...], preferred_element_type=F32).astype(BF16)
        return 0

    lax.fori_loop(0, out.shape[0], one, 0)


def own_blocks(x, weight, after):
    return pl.pallas_call(
        own_kernel,
        out_shape=pltpu.HBM((x.shape[0] // BLOCK, BLOCK, D), BF16),
        in_specs=[VMEM, VMEM, HBM],
        out_specs=VMEM,
        compiler_params=params(16),
        name="project_own",
    )(x, weight, after)


def stats_kernel(x, qw, kw, vw, after, out, keys_sq, values, sums):
    steps = x.shape[0] // CHUNK

    def project(c, carry):
        ksum, qsum = carry
        rows = pl.ds(pl.multiple_of(c * CHUNK, CHUNK), CHUNK)
        part = x[rows, :]
        query = jnp.dot(part, qw[...], preferred_element_type=F32)
        keys = jnp.dot(part, kw[...], preferred_element_type=F32)
        values[rows, :] = jnp.dot(part, vw[...], preferred_element_type=F32)
        keys_sq[rows, :] = keys * keys
        ksum = ksum + jnp.sum(keys * keys, 0, keepdims=True)
        return ksum, qsum + jnp.sum(query * query, 0, keepdims=True)

    zero = jnp.zeros((1, D), F32)
    ksum, qsum = lax.fori_loop(0, steps, project, (zero, zero))
    ktotal = jnp.sum(ksum, 1, keepdims=True)
    qtotal = jnp.sum(qsum, 1, keepdims=True)
    divisor = jnp.where(ktotal > 0, ktotal, 1.0)
    sums[...] = jnp.zeros_like(sums)

    def one(c, _):
        rows = pl.ds(pl.multiple_of(c * CHUNK, CHUNK), CHUNK)
        feat = keys_sq[rows, :] / divisor
        sums[...] += lax.dot_general(
            feat, values[rows, :], (((0,), (0,)), ((), ())),
            precision=HIGHEST, preferred_element_type=F32,
        )
        return 0

    lax.fori_loop(0, steps, one, 0)
    row = lax.broadcasted_iota(jnp.int32, (EXTRA, D), 0)
    extra = jnp.where(row == 0, ksum / divisor, jnp.where(row == 1, ktotal, qtotal))
    out[0:D, :] = sums[...]
    out[D:, :] = extra


def bit_of(step):
    axis, bit = step
    return lax.axis_index(axis) >> bit & 1


def split(rows, extra, bit, keep, away):
    half = rows.shape[0] // 2
    keep[0:half, :] = rows[pl.ds(pl.multiple_of(bit * half, 8), half), :]
    away[0:half, :] = rows[pl.ds(pl.multiple_of((1 - bit) * half, 8), half), :]
    keep[half:half + EXTRA, :] = extra
    away[half:half + EXTRA, :] = extra


def stats(x, qw, kw, vw, after):
    rows = x.shape[0]
    return pl.pallas_call(
        stats_kernel,
        out_shape=jax.ShapeDtypeStruct((D + EXTRA, D), F32),
        in_specs=[VMEM] * 4 + [HBM],
        out_specs=VMEM,
        scratch_shapes=[pltpu.VMEM((rows, D), F32)] * 2 + [pltpu.VMEM((D, D), F32)],
        compiler_params=params(16),
        cost_estimate=cost(rows * D * D * 18, 2 << 20),
        name="attention_sums",
    )(x, qw, kw, vw, after)


def merged(parts):
    rows = parts[0].shape[0] - EXTRA
    extras = [p[rows:, :] for p in parts]
    added = functools.reduce(jnp.add, extras)
    total = added[1:2, :]
    weights = [e[1:2, :] / jnp.where(total > 0, total, 1.0) for e in extras]
    row = lax.broadcasted_iota(jnp.int32, (EXTRA, D), 0)
    extra = jnp.where(row == 0, functools.reduce(jnp.add, [e * w for e, w in zip(extras, weights)]), added)
    return functools.reduce(jnp.add, [p[0:rows, :] * w for p, w in zip(parts, weights)]), extra


def halve_kernel(step, mine, other, keep, away, scratch):
    sums, extra = merged((mine, other))
    scratch[...] = sums
    split(scratch, extra, bit_of(step), keep, away)


def halve(mine, other, step):
    rows = mine.shape[0] - EXTRA
    return pl.pallas_call(
        functools.partial(halve_kernel, step),
        out_shape=(jax.ShapeDtypeStruct((rows // 2 + EXTRA, D), F32),) * 2,
        in_specs=[VMEM, VMEM],
        out_specs=(VMEM, VMEM),
        scratch_shapes=[pltpu.VMEM((rows, D), F32)],
        name="halve_sums",
    )(mine, other)


def merge_kernel(core, *refs):
    out = refs[-1]
    parts = [ref[...] for ref in refs[:-1]]
    if core:
        parts[0] = jnp.where(bit_of(CORE) == 0, parts[0], 0.0)
    sums, extra = merged(parts)
    rows = sums.shape[0]
    out[0:rows, :] = sums
    out[rows:, :] = extra


def merge(*parts, core=False):
    return pl.pallas_call(
        functools.partial(merge_kernel, core),
        out_shape=jax.ShapeDtypeStruct(parts[0].shape, F32),
        in_specs=[VMEM] * len(parts),
        out_specs=VMEM,
        name="merge_sums",
    )(*parts)


def join_kernel(step, mine, other, out):
    rows = mine.shape[0]
    at = bit_of(step)
    out[pl.ds(pl.multiple_of(at * rows, 8), rows), :] = mine[...]
    out[pl.ds(pl.multiple_of((1 - at) * rows, 8), rows), :] = other[...]


def join(mine, other, step):
    return pl.pallas_call(
        functools.partial(join_kernel, step),
        out_shape=jax.ShapeDtypeStruct((2 * mine.shape[0], D), F32),
        in_specs=[VMEM, VMEM],
        out_specs=VMEM,
        name="join_sums",
    )(mine, other)


def swap(x, step):
    axis, bit = step
    return lax.ppermute(x, axis, [(i, i ^ 1 << bit) for i in range(lax.axis_size(axis))])


def partial_sums(mine):
    keep, away = halve(mine, swap(mine, CORE), HALVE[0])
    for done, step in zip(HALVE, HALVE[1:]):
        keep, away = halve(keep, swap(away, done), step)
    return merge(keep, swap(away, HALVE[-1]))


def along_depth(mine):
    span = 2 * DEPTH

    def shift(by):
        return [
            (i, i // span * span + (i + 2 * by[i % 2]) % span)
            for i in range(lax.axis_size("wide"))
            if by[i % 2]
        ]

    return [lax.ppermute(mine, "wide", shift(by)) for by in AROUND]


def whole_sums(mine, others):
    mine = merge(mine, *others, core=True)
    mine = merge(mine, swap(mine, CORE))
    rows, extra = mine[:-EXTRA], mine[-EXTRA:]
    for step in JOIN:
        rows = join(rows, swap(rows, step), step)
    return rows, extra


def plan_kernel(nblocks, first, last, rows, cols, count, local, halo, heads, nexts):
    for out, low, high in ((local, 0, first), (halo, first, last)):
        def clear(r, _):
            heads[r] = -1
            return 0

        lax.fori_loop(0, nblocks, clear, 0)

        def one(t, _):
            c, r = cols[0, t], rows[0, t]

            @pl.when((c >= low) & (c < high))
            def _():
                nexts[t] = heads[r]
                heads[r] = t

            return 0

        lax.fori_loop(0, count[0], one, 0)

        def place(r, n):
            def pair(at):
                t, n = at
                other = nexts[t]
                both = other >= 0
                second = jnp.where(both, other, t)
                out[0, n] = t
                out[1, n] = second
                out[2, n] = cols[0, t] - low
                out[3, n] = cols[0, second] - low
                out[4, n] = both.astype(jnp.int32)
                out[5, n] = r
                return jnp.where(both, nexts[second], -1), n + 1

            return lax.while_loop(lambda at: at[0] >= 0, pair, (heads[r], n))[1]

        n = lax.fori_loop(0, nblocks, place, jnp.int32(0))
        for u in range(PAIRS):
            for line in range(5):
                out[line, n + u] = 0
            out[5, n + u] = nblocks
        out[6, 0] = (n + PAIRS - 1) // PAIRS


def plan(rows, cols, count, nblocks, first, last, after):
    slots = rows.shape[1]
    width = -(-((slots + nblocks) // 2 + PAIRS) // PAIRS) * PAIRS
    shape = jax.ShapeDtypeStruct((8, width), jnp.int32)

    def kernel(rows, cols, count, after, *refs):
        plan_kernel(nblocks, first, last, rows, cols, count, *refs)

    return pl.pallas_call(
        kernel,
        out_shape=(shape, shape),
        in_specs=[SMEM] * 3 + [HBM],
        out_specs=(SMEM, SMEM),
        scratch_shapes=[pltpu.SMEM((nblocks,), jnp.int32), pltpu.SMEM((slots,), jnp.int32)],
        name="plan_tiles",
    )(rows, cols, count, after)


def add_pairs(steps, tiles, two_blocks, acc, before):
    def step(i, _):
        before(i)
        prods = []
        for u in range(PAIRS):
            j = i * PAIRS + u
            second = tiles[steps[1, j]]
            second = jnp.where(steps[4, j] > 0, second, jnp.zeros_like(second))
            both = jnp.concatenate([tiles[steps[0, j]], second], 1)
            prods.append(jnp.dot(both, two_blocks(j), preferred_element_type=F32))
        for u in range(PAIRS):
            r = steps[5, i * PAIRS + u]
            acc[r] = acc[r] + prods[u]
        return 0

    lax.fori_loop(0, steps[6, 0], step, 0)


def local_kernel(nparts, steps, tiles, *refs):
    parts, (base, out, blocks, acc, result, sems) = refs[:nparts], refs[nparts:]
    nblocks = parts[0].shape[0]
    me = lax.axis_index("narrow")
    loads = []
    for by, part in enumerate(parts):
        owner = lax.rem(me + nparts - by, nparts)
        place = blocks.at[pl.ds(owner * nblocks, nblocks)]
        loads.append(pltpu.make_async_copy(part, place, sems.at[by]))
    with_base = base.shape == result.shape
    if with_base:
        loads.append(pltpu.make_async_copy(base, result, sems.at[nparts]))
    for load in loads:
        load.start()
    acc[...] = jnp.zeros_like(acc)
    for load in loads:
        load.wait()
    add_pairs(
        steps, tiles, lambda j: jnp.concatenate([blocks[steps[2, j]], blocks[steps[3, j]]], 0), acc, lambda i: None
    )
    if with_base:
        result[...] = result[...] + acc[:nblocks] / 3.0
    else:
        result[...] = acc[:nblocks]
    store = pltpu.make_async_copy(result, out, sems.at[nparts + 1])
    store.start()
    store.wait()


def local_tiles(steps, tiles, parts, base):
    nblocks = parts[0].shape[0]
    return pl.pallas_call(
        functools.partial(local_kernel, len(parts)),
        out_shape=pltpu.HBM((nblocks, BLOCK, D), F32),
        in_specs=[SMEM, VMEM] + [HBM] * (len(parts) + 1),
        out_specs=HBM,
        scratch_shapes=[
            pltpu.VMEM((len(parts) * nblocks, BLOCK, D), BF16),
            pltpu.VMEM((nblocks + 1, BLOCK, D), F32),
            pltpu.VMEM((nblocks, BLOCK, D), F32),
            pltpu.SemaphoreType.DMA((len(parts) + 2,)),
        ],
        compiler_params=params(20),
        cost_estimate=cost(48 * BLOCK * BLOCK * D * 2, 9 << 20),
        name="local_tiles",
    )(steps, tiles, *map(in_hbm, parts), in_hbm(base))


def load_halo(steps, blocks, got, sems):
    def one(i, _):
        for u in range(PAIRS):
            j = i * PAIRS + u
            for half in range(2):
                place = got.at[j, pl.ds(half * BLOCK, BLOCK)]
                pltpu.make_async_copy(blocks.at[steps[2 + half, j]], place, sems.at[i]).start()
        return 0

    lax.fori_loop(0, steps[6, 0], one, 0)


def add_halo(steps, tiles, got, acc, sems):
    def before(i):
        at = pl.ds(i * PAIRS, PAIRS)
        pltpu.make_async_copy(got.at[at], got.at[at], sems.at[i]).wait()

    add_pairs(steps, tiles, lambda j: got[j], acc, before)


def halo_scratch(steps, part):
    nblocks = part.shape[0]
    return [
        pltpu.VMEM((steps.shape[1], 2 * BLOCK, D), BF16),
        pltpu.VMEM((nblocks + 1, BLOCK, D), F32),
        pltpu.VMEM(part.shape, F32),
        pltpu.SemaphoreType.DMA((steps.shape[1] // PAIRS + nblocks // NORM,)),
    ]


def pieces_of(source, target, sems):
    count = source.shape[0] // NORM

    def piece(i):
        at = pl.ds(i * NORM, NORM)
        return pltpu.make_async_copy(source.at[at], target.at[at], sems.at[sems.shape[0] - count + i])

    return piece, count


def hop_kernel(send, steps, tiles, blocks, part, *refs):
    h_out, out, got, acc, local, loads, h_own, zeros, heads, nexts, sems = refs[len(AROUND):]
    nblocks = h_own.shape[0]
    load_halo(steps, blocks, got, loads)
    piece, count = pieces_of(part, local, loads)
    for i in range(count):
        piece(i).start()
    send_order(send, heads, nexts, zeros, out, sems.at[1])
    acc[...] = jnp.zeros_like(acc)
    add_halo(steps, tiles, got, acc, loads)

    def some(i, _):
        piece(i).wait()
        for u in range(NORM):
            b = i * NORM + u
            h_own[b] = (acc[b] + local[b]).astype(BF16)
        for u in range(NORM):
            send_block(i * NORM + u, h_own, heads, nexts, h_out, out, sems)
        return 0

    lax.fori_loop(0, count, some, 0)
    wait_sent(h_own, h_out, out, sems)


def hop(send, steps, tiles, blocks, part, after):
    nblocks = part.shape[0]
    return pl.pallas_call(
        hop_kernel,
        out_shape=(pltpu.HBM((nblocks, BLOCK, D), BF16), pltpu.HBM(blocks.shape, BF16)),
        in_specs=[SMEM, SMEM, VMEM, HBM, HBM] + [HBM] * len(after),
        out_specs=(HBM, HBM),
        scratch_shapes=halo_scratch(steps, part) + send_scratch(nblocks, blocks.shape[0]),
        compiler_params=params(20),
        name="halo_tiles_send",
    )(send, steps, tiles, in_hbm(blocks), in_hbm(part), *after)


def attention_kernel(total, x, qw, vw, kv_sums, extra, hop_zero, hop_one, out, kv):
    width = float(D)
    each = D >> len(HALVE)
    for place in range(1 << len(HALVE)):
        bits = {step: place >> at & 1 for at, step in enumerate(HALVE[::-1])}
        came = sum(bits[step] << at for at, step in enumerate(JOIN))
        kv[place * each:(place + 1) * each, :] = kv_sums[came * each:(came + 1) * each, :] * width
    key_mean = extra[0:1, :] * width
    scale = total * width / extra[2:3, :]

    def one(c, _):
        rows = pl.ds(pl.multiple_of(c * CHUNK, CHUNK), CHUNK)
        part = x[rows, :]
        query = jnp.dot(part, qw[...], preferred_element_type=F32)
        values = jnp.dot(part, vw[...], preferred_element_type=F32)
        feat = query * query * scale
        numer = jnp.dot(feat, kv[...], precision=HIGHEST, preferred_element_type=F32) + width * values
        denom = jnp.sum(feat * key_mean, 1, keepdims=True) + width
        graph = hop_zero[rows, :].astype(F32) + hop_one[rows, :].astype(F32)
        out[rows, :] = numer / denom + graph / 3.0
        return 0

    lax.fori_loop(0, x.shape[0] // CHUNK, one, 0)


def attention(total, x, qw, vw, kv_sums, extra, hop_zero, hop_one):
    rows = x.shape[0]
    return pl.pallas_call(
        functools.partial(attention_kernel, total),
        out_shape=pltpu.HBM((rows, D), F32),
        in_specs=[VMEM] * 7,
        out_specs=VMEM,
        scratch_shapes=[pltpu.VMEM((D, D), F32)],
        compiler_params=params(16),
        cost_estimate=cost(rows * D * D * 18, 6 << 20),
        name="attention",
    )(x, qw, vw, kv_sums, extra, hop_zero, hop_one)


def finish_kernel(steps, tiles, blocks, base, gain, out, got, acc, mixing, loads, done, sem):
    nblocks = base.shape[0]
    load_halo(steps, blocks, got, loads)
    piece, count = pieces_of(base, mixing, loads)
    for i in range(count):
        piece(i).start()
    acc[...] = jnp.zeros_like(acc)
    add_halo(steps, tiles, got, acc, loads)

    def some(i, _):
        piece(i).wait()
        for u in range(NORM):
            b = i * NORM + u
            mixed = mixing[b] + acc[b] / 3.0
            center = mixed - jnp.mean(mixed, 1, keepdims=True)
            scale = lax.rsqrt(jnp.mean(center * center, 1, keepdims=True) + 1e-05)
            done[b] = (gain[...] * center * scale).astype(BF16)
        at = pl.ds(i * NORM, NORM)
        pltpu.make_async_copy(done.at[at], out.at[at], sem).start()
        return 0

    lax.fori_loop(0, count, some, 0)
    pltpu.make_async_copy(done, out, sem).wait()


def finish(steps, tiles, blocks, base, gain):
    nblocks = base.shape[0]
    return pl.pallas_call(
        finish_kernel,
        out_shape=jax.ShapeDtypeStruct((nblocks, BLOCK, D), BF16),
        in_specs=[SMEM, VMEM, HBM, HBM, VMEM],
        out_specs=HBM,
        scratch_shapes=halo_scratch(steps, base) + [
            pltpu.VMEM((nblocks, BLOCK, D), BF16), pltpu.SemaphoreType.DMA,
        ],
        compiler_params=params(20),
        name="halo_tiles_norm",
    )(steps, tiles, in_hbm(blocks), in_hbm(base), gain)


def group_blocks(own):
    groups = lax.axis_size("narrow")
    return [own] + [
        lax.ppermute(own, "narrow", [(i, (i + by) % groups) for i in range(groups)])
        for by in range(1, groups)
    ]


def shards(x, qw, kw, vw, gw, gain, tiles, tile_rows, tile_cols, tile_count, send_list):
    rows_dev = x.shape[0]
    nblocks = rows_dev // BLOCK
    peers, groups = lax.axis_size("wide"), lax.axis_size("narrow")
    total = float(rows_dev * peers * groups)
    first = groups * nblocks

    outgoing = start(send_list, x, gw, peers)
    hop_zero = own_blocks(x, gw, outgoing)
    received = lax.all_to_all(outgoing, "wide", 0, 0, tiled=True)
    group = group_blocks(hop_zero)
    mine = partial_sums(stats(x, qw, kw, vw, hop_zero))
    others = along_depth(mine)
    local, halo = plan(tile_rows, tile_cols, tile_count, nblocks, first, first + peers, hop_zero)
    part = local_tiles(local, tiles, group, mine)
    hop_one, outgoing = hop(send_list, halo, tiles, received, part, others)
    received = lax.all_to_all(outgoing, "wide", 0, 0, tiled=True)
    group = group_blocks(hop_one)
    kv_sums, extra = whole_sums(mine, others)
    base = attention(
        total, x, qw, vw, kv_sums, extra, hop_zero.reshape(rows_dev, D), hop_one.reshape(rows_dev, D)
    )
    base = local_tiles(local, tiles, group, base.reshape(nblocks, BLOCK, D))
    out = finish(halo, tiles, received, base, gain[None, :])
    return out.reshape(rows_dev, D)


def solution(mesh):
    return jax.shard_map(
        shards,
        mesh=mesh,
        in_specs=(
            P(("wide", "narrow"), None),
            P(),
            P(),
            P(),
            P(),
            P(),
            P(("wide", "narrow"), None, None),
            P(("wide", "narrow"), None),
            P(("wide", "narrow"), None),
            P(("wide", "narrow")),
            P(("wide", "narrow"), None),
        ),
        out_specs=P(("wide", "narrow"), None),
        check_vma=False,
    )
```

```python
import functools

import jax
import jax.numpy as jnp
from jax import lax
from jax.experimental import pallas as pl
from jax.experimental.pallas import tpu as pltpu
from jax.sharding import PartitionSpec as P

D = 256
BLOCK = 128
PAIRS = 8
CHUNK = 256
NORM = 4
EXTRA = 8
CORE = ("wide", 0)
HALVE = (("wide", 4), ("wide", 5), ("narrow", 0), ("narrow", 1))
DEPTH = 8
AROUND = ((2, 4), (6, 3), (1, 5), (7, 0))
JOIN = (("wide", 5), ("wide", 4), ("narrow", 1), ("narrow", 0))
F32 = jnp.float32
BF16 = jnp.bfloat16
HIGHEST = lax.Precision.HIGHEST
SMEM = pl.BlockSpec(memory_space=pltpu.SMEM)
VMEM = pl.BlockSpec(memory_space=pltpu.VMEM)
HBM = pl.BlockSpec(memory_space=pltpu.HBM)


def in_hbm(x):
    return pltpu.with_memory_space_constraint(x, pltpu.HBM)


def params(mib):
    return pltpu.CompilerParams(vmem_limit_bytes=mib << 20)


def cost(flops, nbytes):
    return pl.CostEstimate(flops=flops, bytes_accessed=nbytes, transcendentals=0)


def send_order(send, heads, nexts, zeros, out, sem):
    zeros[...] = jnp.zeros_like(zeros)

    def clear(b, _):
        heads[b] = -1
        return 0

    lax.fori_loop(0, heads.shape[0], clear, 0)

    def one(w, _):
        index = send[0, w]
        block = jnp.maximum(index, 0)

        @pl.when(index >= 0)
        def _():
            nexts[w] = heads[block]
            heads[block] = w

        @pl.when(index < 0)
        def _():
            pltpu.make_async_copy(zeros, out.at[w], sem).start()

        return 0

    lax.fori_loop(0, nexts.shape[0], one, 0)


def send_block(b, src, heads, nexts, h_out, out, sems):
    if h_out is not None:
        pltpu.make_async_copy(src.at[b], h_out.at[b], sems.at[0]).start()

    def one(w):
        pltpu.make_async_copy(src.at[b], out.at[w], sems.at[1]).start()
        return nexts[w]

    lax.while_loop(lambda w: w >= 0, one, heads[b])


def wait_sent(src, h_out, out, sems):
    if h_out is not None:
        pltpu.make_async_copy(src, h_out, sems.at[0]).wait()
    pltpu.make_async_copy(out, out, sems.at[1]).wait()


def send_scratch(nblocks, peers):
    return [
        pltpu.VMEM((nblocks, BLOCK, D), BF16),
        pltpu.VMEM((BLOCK, D), BF16),
        pltpu.SMEM((nblocks,), jnp.int32),
        pltpu.SMEM((peers,), jnp.int32),
        pltpu.SemaphoreType.DMA((2,)),
    ]


def start_kernel(send, x, weight, out, h_own, zeros, heads, nexts, sems, send_own, x_own, weight_own, loads):
    pieces = loads.shape[0] - 2
    rows = x.shape[0] // pieces
    per = rows // BLOCK
    sends = pltpu.make_async_copy(send, send_own, loads.at[0])
    weights = pltpu.make_async_copy(weight, weight_own, loads.at[1])
    sends.start()
    weights.start()
    parts = [
        pltpu.make_async_copy(x.at[pl.ds(p * rows, rows)], x_own.at[pl.ds(p * rows, rows)], loads.at[2 + p])
        for p in range(pieces)
    ]
    for part in parts:
        part.start()
    sends.wait()
    send_order(send_own, heads, nexts, zeros, out, sems.at[1])
    weights.wait()
    for p in range(pieces):
        parts[p].wait()
        for b in range(p * per, (p + 1) * per):
            h_own[b] = jnp.dot(
                x_own[b * BLOCK:(b + 1) * BLOCK, :], weight_own[...], preferred_element_type=F32
            ).astype(BF16)
        for b in range(p * per, (p + 1) * per):
            send_block(b, h_own, heads, nexts, None, out, sems)
    wait_sent(h_own, None, out, sems)


def start(send, x, weight, peers):
    nblocks = x.shape[0] // BLOCK
    pieces = 4
    return pl.pallas_call(
        start_kernel,
        out_shape=pltpu.HBM((peers, BLOCK, D), BF16),
        in_specs=[HBM] * 3,
        out_specs=HBM,
        scratch_shapes=send_scratch(nblocks, peers) + [
            pltpu.SMEM(send.shape, jnp.int32),
            pltpu.VMEM(x.shape, BF16),
            pltpu.VMEM(weight.shape, BF16),
            pltpu.SemaphoreType.DMA((pieces + 2,)),
        ],
        compiler_params=params(16),
        name="project_send",
    )(in_hbm(send), in_hbm(x), in_hbm(weight))


def own_kernel(x, weight, after, out):
    def one(b, _):
        rows = pl.ds(pl.multiple_of(b * BLOCK, BLOCK), BLOCK)
        out[b] = jnp.dot(x[rows, :], weight[...], preferred_element_type=F32).astype(BF16)
        return 0

    lax.fori_loop(0, out.shape[0], one, 0)


def own_blocks(x, weight, after):
    return pl.pallas_call(
        own_kernel,
        out_shape=pltpu.HBM((x.shape[0] // BLOCK, BLOCK, D), BF16),
        in_specs=[VMEM, VMEM, HBM],
        out_specs=VMEM,
        compiler_params=params(16),
        name="project_own",
    )(x, weight, after)


def stats_kernel(x, qw, kw, vw, after, out, keys_sq, values, sums):
    steps = x.shape[0] // CHUNK

    def project(c, carry):
        ksum, qsum = carry
        rows = pl.ds(pl.multiple_of(c * CHUNK, CHUNK), CHUNK)
        part = x[rows, :]
        query = jnp.dot(part, qw[...], preferred_element_type=F32)
        keys = jnp.dot(part, kw[...], preferred_element_type=F32)
        values[rows, :] = jnp.dot(part, vw[...], preferred_element_type=F32)
        keys_sq[rows, :] = keys * keys
        ksum = ksum + jnp.sum(keys * keys, 0, keepdims=True)
        return ksum, qsum + jnp.sum(query * query, 0, keepdims=True)

    zero = jnp.zeros((1, D), F32)
    ksum, qsum = lax.fori_loop(0, steps, project, (zero, zero))
    ktotal = jnp.sum(ksum, 1, keepdims=True)
    qtotal = jnp.sum(qsum, 1, keepdims=True)
    divisor = jnp.where(ktotal > 0, ktotal, 1.0)
    sums[...] = jnp.zeros_like(sums)

    def one(c, _):
        rows = pl.ds(pl.multiple_of(c * CHUNK, CHUNK), CHUNK)
        feat = keys_sq[rows, :] / divisor
        sums[...] += lax.dot_general(
            feat, values[rows, :], (((0,), (0,)), ((), ())),
            precision=HIGHEST, preferred_element_type=F32,
        )
        return 0

    lax.fori_loop(0, steps, one, 0)
    row = lax.broadcasted_iota(jnp.int32, (EXTRA, D), 0)
    extra = jnp.where(row == 0, ksum / divisor, jnp.where(row == 1, ktotal, qtotal))
    out[0:D, :] = sums[...]
    out[D:, :] = extra


def bit_of(step):
    axis, bit = step
    return lax.axis_index(axis) >> bit & 1


def split(rows, extra, bit, keep, away):
    half = rows.shape[0] // 2
    keep[0:half, :] = rows[pl.ds(pl.multiple_of(bit * half, 8), half), :]
    away[0:half, :] = rows[pl.ds(pl.multiple_of((1 - bit) * half, 8), half), :]
    keep[half:half + EXTRA, :] = extra
    away[half:half + EXTRA, :] = extra


def stats(x, qw, kw, vw, after):
    rows = x.shape[0]
    return pl.pallas_call(
        stats_kernel,
        out_shape=jax.ShapeDtypeStruct((D + EXTRA, D), F32),
        in_specs=[VMEM] * 4 + [HBM],
        out_specs=VMEM,
        scratch_shapes=[pltpu.VMEM((rows, D), F32)] * 2 + [pltpu.VMEM((D, D), F32)],
        compiler_params=params(16),
        cost_estimate=cost(rows * D * D * 18, 2 << 20),
        name="attention_sums",
    )(x, qw, kw, vw, after)


def merged(parts):
    rows = parts[0].shape[0] - EXTRA
    extras = [p[rows:, :] for p in parts]
    added = functools.reduce(jnp.add, extras)
    total = added[1:2, :]
    weights = [e[1:2, :] / jnp.where(total > 0, total, 1.0) for e in extras]
    row = lax.broadcasted_iota(jnp.int32, (EXTRA, D), 0)
    extra = jnp.where(row == 0, functools.reduce(jnp.add, [e * w for e, w in zip(extras, weights)]), added)
    return functools.reduce(jnp.add, [p[0:rows, :] * w for p, w in zip(parts, weights)]), extra


def halve_kernel(step, mine, other, keep, away, scratch):
    sums, extra = merged((mine, other))
    scratch[...] = sums
    split(scratch, extra, bit_of(step), keep, away)


def halve(mine, other, step):
    rows = mine.shape[0] - EXTRA
    return pl.pallas_call(
        functools.partial(halve_kernel, step),
        out_shape=(jax.ShapeDtypeStruct((rows // 2 + EXTRA, D), F32),) * 2,
        in_specs=[VMEM, VMEM],
        out_specs=(VMEM, VMEM),
        scratch_shapes=[pltpu.VMEM((rows, D), F32)],
        name="halve_sums",
    )(mine, other)


def merge_kernel(core, *refs):
    out = refs[-1]
    parts = [ref[...] for ref in refs[:-1]]
    if core:
        parts[0] = jnp.where(bit_of(CORE) == 0, parts[0], 0.0)
    sums, extra = merged(parts)
    rows = sums.shape[0]
    out[0:rows, :] = sums
    out[rows:, :] = extra


def merge(*parts, core=False):
    return pl.pallas_call(
        functools.partial(merge_kernel, core),
        out_shape=jax.ShapeDtypeStruct(parts[0].shape, F32),
        in_specs=[VMEM] * len(parts),
        out_specs=VMEM,
        name="merge_sums",
    )(*parts)


def join_kernel(step, mine, other, out):
    rows = mine.shape[0]
    at = bit_of(step)
    out[pl.ds(pl.multiple_of(at * rows, 8), rows), :] = mine[...]
    out[pl.ds(pl.multiple_of((1 - at) * rows, 8), rows), :] = other[...]


def join(mine, other, step):
    return pl.pallas_call(
        functools.partial(join_kernel, step),
        out_shape=jax.ShapeDtypeStruct((2 * mine.shape[0], D), F32),
        in_specs=[VMEM, VMEM],
        out_specs=VMEM,
        name="join_sums",
    )(mine, other)


def swap(x, step):
    axis, bit = step
    return lax.ppermute(x, axis, [(i, i ^ 1 << bit) for i in range(lax.axis_size(axis))])


def partial_sums(mine):
    keep, away = halve(mine, swap(mine, CORE), HALVE[0])
    for done, step in zip(HALVE, HALVE[1:]):
        keep, away = halve(keep, swap(away, done), step)
    return merge(keep, swap(away, HALVE[-1]))


def along_depth(mine):
    span = 2 * DEPTH

    def shift(by):
        return [
            (i, i // span * span + (i + 2 * by[i % 2]) % span)
            for i in range(lax.axis_size("wide"))
            if by[i % 2]
        ]

    return [lax.ppermute(mine, "wide", shift(by)) for by in AROUND]


def whole_sums(mine, others):
    mine = merge(mine, *others, core=True)
    mine = merge(mine, swap(mine, CORE))
    rows, extra = mine[:-EXTRA], mine[-EXTRA:]
    for step in JOIN:
        rows = join(rows, swap(rows, step), step)
    return rows, extra


def plan_kernel(nblocks, first, last, rows, cols, count, local, halo, heads, nexts):
    for out, low, high in ((local, 0, first), (halo, first, last)):
        def clear(r, _):
            heads[r] = -1
            return 0

        lax.fori_loop(0, nblocks, clear, 0)

        def one(t, _):
            c, r = cols[0, t], rows[0, t]

            @pl.when((c >= low) & (c < high))
            def _():
                nexts[t] = heads[r]
                heads[r] = t

            return 0

        lax.fori_loop(0, count[0], one, 0)

        def place(r, n):
            def pair(at):
                t, n = at
                other = nexts[t]
                both = other >= 0
                second = jnp.where(both, other, t)
                out[0, n] = t
                out[1, n] = second
                out[2, n] = cols[0, t] - low
                out[3, n] = cols[0, second] - low
                out[4, n] = both.astype(jnp.int32)
                out[5, n] = r
                return jnp.where(both, nexts[second], -1), n + 1

            return lax.while_loop(lambda at: at[0] >= 0, pair, (heads[r], n))[1]

        n = lax.fori_loop(0, nblocks, place, jnp.int32(0))
        for u in range(PAIRS):
            for line in range(5):
                out[line, n + u] = 0
            out[5, n + u] = nblocks
        out[6, 0] = (n + PAIRS - 1) // PAIRS


def plan(rows, cols, count, nblocks, first, last, after):
    slots = rows.shape[1]
    width = -(-((slots + nblocks) // 2 + PAIRS) // PAIRS) * PAIRS
    shape = jax.ShapeDtypeStruct((8, width), jnp.int32)

    def kernel(rows, cols, count, after, *refs):
        plan_kernel(nblocks, first, last, rows, cols, count, *refs)

    return pl.pallas_call(
        kernel,
        out_shape=(shape, shape),
        in_specs=[SMEM] * 3 + [HBM],
        out_specs=(SMEM, SMEM),
        scratch_shapes=[pltpu.SMEM((nblocks,), jnp.int32), pltpu.SMEM((slots,), jnp.int32)],
        name="plan_tiles",
    )(rows, cols, count, after)


def add_pairs(steps, tiles, two_blocks, acc, before):
    def step(i, _):
        before(i)
        prods = []
        for u in range(PAIRS):
            j = i * PAIRS + u
            second = tiles[steps[1, j]]
            second = jnp.where(steps[4, j] > 0, second, jnp.zeros_like(second))
            both = jnp.concatenate([tiles[steps[0, j]], second], 1)
            prods.append(jnp.dot(both, two_blocks(j), preferred_element_type=F32))
        for u in range(PAIRS):
            r = steps[5, i * PAIRS + u]
            acc[r] = acc[r] + prods[u]
        return 0

    lax.fori_loop(0, steps[6, 0], step, 0)


def local_kernel(nparts, steps, tiles, *refs):
    parts, (base, out, blocks, acc, result, sems) = refs[:nparts], refs[nparts:]
    nblocks = parts[0].shape[0]
    me = lax.axis_index("narrow")
    loads = []
    for by, part in enumerate(parts):
        owner = lax.rem(me + nparts - by, nparts)
        place = blocks.at[pl.ds(owner * nblocks, nblocks)]
        loads.append(pltpu.make_async_copy(part, place, sems.at[by]))
    with_base = base.shape == result.shape
    if with_base:
        loads.append(pltpu.make_async_copy(base, result, sems.at[nparts]))
    for load in loads:
        load.start()
    acc[...] = jnp.zeros_like(acc)
    for load in loads:
        load.wait()
    add_pairs(
        steps, tiles, lambda j: jnp.concatenate([blocks[steps[2, j]], blocks[steps[3, j]]], 0), acc, lambda i: None
    )
    if with_base:
        result[...] = result[...] + acc[:nblocks] / 3.0
    else:
        result[...] = acc[:nblocks]
    store = pltpu.make_async_copy(result, out, sems.at[nparts + 1])
    store.start()
    store.wait()


def local_tiles(steps, tiles, parts, base):
    nblocks = parts[0].shape[0]
    return pl.pallas_call(
        functools.partial(local_kernel, len(parts)),
        out_shape=pltpu.HBM((nblocks, BLOCK, D), F32),
        in_specs=[SMEM, VMEM] + [HBM] * (len(parts) + 1),
        out_specs=HBM,
        scratch_shapes=[
            pltpu.VMEM((len(parts) * nblocks, BLOCK, D), BF16),
            pltpu.VMEM((nblocks + 1, BLOCK, D), F32),
            pltpu.VMEM((nblocks, BLOCK, D), F32),
            pltpu.SemaphoreType.DMA((len(parts) + 2,)),
        ],
        compiler_params=params(24),
        cost_estimate=cost(48 * BLOCK * BLOCK * D * 2, 9 << 20),
        name="local_tiles",
    )(steps, tiles, *map(in_hbm, parts), in_hbm(base))


def load_halo(steps, blocks, got, sems):
    def one(i, _):
        for u in range(PAIRS):
            j = i * PAIRS + u
            for half in range(2):
                place = got.at[j, pl.ds(half * BLOCK, BLOCK)]
                pltpu.make_async_copy(blocks.at[steps[2 + half, j]], place, sems.at[i]).start()
        return 0

    lax.fori_loop(0, steps[6, 0], one, 0)


def add_halo(steps, tiles, got, acc, sems):
    def before(i):
        at = pl.ds(i * PAIRS, PAIRS)
        pltpu.make_async_copy(got.at[at], got.at[at], sems.at[i]).wait()

    add_pairs(steps, tiles, lambda j: got[j], acc, before)


def halo_scratch(steps, part):
    nblocks = part.shape[0]
    return [
        pltpu.VMEM((steps.shape[1], 2 * BLOCK, D), BF16),
        pltpu.VMEM((nblocks + 1, BLOCK, D), F32),
        pltpu.VMEM(part.shape, F32),
        pltpu.SemaphoreType.DMA((steps.shape[1] // PAIRS + nblocks // NORM,)),
    ]


def pieces_of(source, target, sems):
    count = source.shape[0] // NORM

    def piece(i):
        at = pl.ds(i * NORM, NORM)
        return pltpu.make_async_copy(source.at[at], target.at[at], sems.at[sems.shape[0] - count + i])

    return piece, count


def hop_kernel(send, steps, tiles, blocks, part, *refs):
    h_out, out, got, acc, local, loads, h_own, zeros, heads, nexts, sems = refs[len(AROUND):]
    nblocks = h_own.shape[0]
    load_halo(steps, blocks, got, loads)
    piece, count = pieces_of(part, local, loads)
    for i in range(count):
        piece(i).start()
    send_order(send, heads, nexts, zeros, out, sems.at[1])
    acc[...] = jnp.zeros_like(acc)
    add_halo(steps, tiles, got, acc, loads)

    def some(i, _):
        piece(i).wait()
        for u in range(NORM):
            b = i * NORM + u
            h_own[b] = (acc[b] + local[b]).astype(BF16)
        for u in range(NORM):
            send_block(i * NORM + u, h_own, heads, nexts, h_out, out, sems)
        return 0

    lax.fori_loop(0, count, some, 0)
    wait_sent(h_own, h_out, out, sems)


def hop(send, steps, tiles, blocks, part, after):
    nblocks = part.shape[0]
    return pl.pallas_call(
        hop_kernel,
        out_shape=(pltpu.HBM((nblocks, BLOCK, D), BF16), pltpu.HBM(blocks.shape, BF16)),
        in_specs=[SMEM, SMEM, VMEM, HBM, HBM] + [HBM] * len(after),
        out_specs=(HBM, HBM),
        scratch_shapes=halo_scratch(steps, part) + send_scratch(nblocks, blocks.shape[0]),
        compiler_params=params(24),
        name="halo_tiles_send",
    )(send, steps, tiles, in_hbm(blocks), in_hbm(part), *after)


def attention_kernel(total, x, qw, vw, kv_sums, extra, hop_zero, hop_one, out, kv):
    width = float(D)
    each = D >> len(HALVE)
    for place in range(1 << len(HALVE)):
        bits = {step: place >> at & 1 for at, step in enumerate(HALVE[::-1])}
        came = sum(bits[step] << at for at, step in enumerate(JOIN))
        kv[place * each:(place + 1) * each, :] = kv_sums[came * each:(came + 1) * each, :] * width
    key_mean = extra[0:1, :] * width
    scale = total * width / extra[2:3, :]

    def one(c, _):
        rows = pl.ds(pl.multiple_of(c * CHUNK, CHUNK), CHUNK)
        part = x[rows, :]
        query = jnp.dot(part, qw[...], preferred_element_type=F32)
        values = jnp.dot(part, vw[...], preferred_element_type=F32)
        feat = query * query * scale
        numer = jnp.dot(feat, kv[...], precision=HIGHEST, preferred_element_type=F32) + width * values
        denom = jnp.sum(feat * key_mean, 1, keepdims=True) + width
        graph = hop_zero[rows, :].astype(F32) + hop_one[rows, :].astype(F32)
        out[rows, :] = numer / denom + graph / 3.0
        return 0

    lax.fori_loop(0, x.shape[0] // CHUNK, one, 0)


def attention(total, x, qw, vw, kv_sums, extra, hop_zero, hop_one):
    rows = x.shape[0]
    return pl.pallas_call(
        functools.partial(attention_kernel, total),
        out_shape=pltpu.HBM((rows, D), F32),
        in_specs=[VMEM] * 7,
        out_specs=VMEM,
        scratch_shapes=[pltpu.VMEM((D, D), F32)],
        compiler_params=params(16),
        cost_estimate=cost(rows * D * D * 18, 6 << 20),
        name="attention",
    )(x, qw, vw, kv_sums, extra, hop_zero, hop_one)


def finish_kernel(steps, tiles, blocks, base, gain, out, got, acc, mixing, loads, done, sem):
    nblocks = base.shape[0]
    load_halo(steps, blocks, got, loads)
    piece, count = pieces_of(base, mixing, loads)
    for i in range(count):
        piece(i).start()
    acc[...] = jnp.zeros_like(acc)
    add_halo(steps, tiles, got, acc, loads)

    def some(i, _):
        piece(i).wait()
        for u in range(NORM):
            b = i * NORM + u
            mixed = mixing[b] + acc[b] / 3.0
            center = mixed - jnp.mean(mixed, 1, keepdims=True)
            scale = lax.rsqrt(jnp.mean(center * center, 1, keepdims=True) + 1e-05)
            done[b] = (gain[...] * center * scale).astype(BF16)
        at = pl.ds(i * NORM, NORM)
        pltpu.make_async_copy(done.at[at], out.at[at], sem).start()
        return 0

    lax.fori_loop(0, count, some, 0)
    pltpu.make_async_copy(done, out, sem).wait()


def finish(steps, tiles, blocks, base, gain):
    nblocks = base.shape[0]
    return pl.pallas_call(
        finish_kernel,
        out_shape=jax.ShapeDtypeStruct((nblocks, BLOCK, D), BF16),
        in_specs=[SMEM, VMEM, HBM, HBM, VMEM],
        out_specs=HBM,
        scratch_shapes=halo_scratch(steps, base) + [
            pltpu.VMEM((nblocks, BLOCK, D), BF16), pltpu.SemaphoreType.DMA,
        ],
        compiler_params=params(24),
        name="halo_tiles_norm",
    )(steps, tiles, in_hbm(blocks), in_hbm(base), gain)


def group_blocks(own):
    groups = lax.axis_size("narrow")
    return [own] + [
        lax.ppermute(own, "narrow", [(i, (i + by) % groups) for i in range(groups)])
        for by in range(1, groups)
    ]


def shards(x, qw, kw, vw, gw, gain, tiles, tile_rows, tile_cols, tile_count, send_list):
    rows_dev = x.shape[0]
    nblocks = rows_dev // BLOCK
    peers, groups = lax.axis_size("wide"), lax.axis_size("narrow")
    total = float(rows_dev * peers * groups)
    first = groups * nblocks

    outgoing = start(send_list, x, gw, peers)
    hop_zero = own_blocks(x, gw, outgoing)
    received = lax.all_to_all(outgoing, "wide", 0, 0, tiled=True)
    group = group_blocks(hop_zero)
    mine = partial_sums(stats(x, qw, kw, vw, hop_zero))
    others = along_depth(mine)
    local, halo = plan(tile_rows, tile_cols, tile_count, nblocks, first, first + peers, hop_zero)
    part = local_tiles(local, tiles, group, mine)
    hop_one, outgoing = hop(send_list, halo, tiles, received, part, others)
    received = lax.all_to_all(outgoing, "wide", 0, 0, tiled=True)
    group = group_blocks(hop_one)
    kv_sums, extra = whole_sums(mine, others)
    base = attention(
        total, x, qw, vw, kv_sums, extra, hop_zero.reshape(rows_dev, D), hop_one.reshape(rows_dev, D)
    )
    base = local_tiles(local, tiles, group, base.reshape(nblocks, BLOCK, D))
    out = finish(halo, tiles, received, base, gain[None, :])
    return out.reshape(rows_dev, D)


def solution(mesh):
    return jax.shard_map(
        shards,
        mesh=mesh,
        in_specs=(
            P(("wide", "narrow"), None),
            P(),
            P(),
            P(),
            P(),
            P(),
            P(("wide", "narrow"), None, None),
            P(("wide", "narrow"), None),
            P(("wide", "narrow"), None),
            P(("wide", "narrow")),
            P(("wide", "narrow"), None),
        ),
        out_specs=P(("wide", "narrow"), None),
        check_vma=False,
    )
```
